32 devices in a mesh: grp: 1, blk: 32 (over z, y, x, core).
Axes of the slice: x: 2, y: 2, z: 4, core: 2. Of those that a mesh axis runs over, the one named last changes fastest.
Arguments:
- sigma_anc: float32 [16384, 16384], P('grp', 'blk')
- panels: float32 [16384, 1024], P(('grp', 'blk')), may hold values from -0.0625 to 0.0625
- diag_inv: float32 [1024, 256], replicated, may hold values from -6 to 6
- scaled_parent_panel: float32 [512, 256], replicated, may hold values from -0.375 to 0.375
- struct_upper: int32 [2, 32], replicated, may hold values from 0 to 63, as said below
- struct_lower: int32 [2, 16], replicated, may hold values from 0 to 63, as said below
Outputs:
- cov_panel: float32 [16384, 1024], P(('blk', 'grp'))
- cov_diag: float32 [1024, 256], P('blk')
- cov_parent: float32 [512, 256], P('blk')
The draws below stay inside these ranges and needn't reach their ends.
Inputs may be any that keep to these rules, and one draw needn't show every extreme that they name: `struct_upper`: each row lists 32 different ancestor blocks. `struct_lower`: each row lists 16 different blocks, all in its parent's row of struct_upper.
All inputs are finite; a program needn't handle non-finite values.
Results may differ from the reference program's by a relative error of at most 0.00011.
Values sent between devices are 32-bit elements; how exact they have to be, the bound alone decides.
No kernel may reach another device: no remote copies, remote signals or barrier semaphores. Data moves between devices by JAX's collectives and lax.ppermute only.
A program may use at most 192 MiB of HBM per device.

```python
import math
import jax
import jax.numpy as jnp
from jax import lax

NODE_WIDTH = 256
UPPER_NODES_1 = 2
LOWER_NODES_2 = 2
NS = 4
ANCESTOR_COLUMNS = 16384
NA = 64
K1 = 32
K2 = 16


def structure_all(key):
    keys_up = jax.random.split(jax.random.fold_in(key, 11), UPPER_NODES_1)
    lists_up = jax.vmap(lambda k: jax.random.permutation(k, NA)[:K1])(keys_up).astype(jnp.int32)
    parent_ids = (jnp.arange(LOWER_NODES_2, dtype=jnp.int32) % UPPER_NODES_1).astype(jnp.int32)
    keys_low = jax.random.split(jax.random.fold_in(key, 13), LOWER_NODES_2)
    picks = jax.vmap(lambda k: jax.random.permutation(k, K1)[:K2])(keys_low).astype(jnp.int32)
    lists_low = jnp.take_along_axis(lists_up[parent_ids], picks, axis=1).astype(jnp.int32)
    return (lists_up, lists_low)


def draw_struct_upper(key, part):
    return structure_all(key)[0]


def draw_struct_lower(key, part):
    return structure_all(key)[1]


def draw_sigma_anc(key, part):
    base = jax.random.normal(key, (ANCESTOR_COLUMNS, ANCESTOR_COLUMNS), jnp.float32)
    sym = (base + base.T) * math.sqrt(0.5)
    return sym.astype(jnp.float32)


def block_levels(rng, shape, cuts, low, top_value):
    def one(position, blocks):
        steps = jax.random.uniform(jax.random.fold_in(jax.random.fold_in(rng, 6), position), (blocks,), jnp.float32, low / len(cuts), top_value / len(cuts))
        return jnp.repeat(jnp.exp(steps), shape[position] // blocks).reshape((-1,) + (1,) * (len(shape) - position - 1))

    factor_of = one(*cuts[0])
    for cut in cuts[1:]:
        factor_of = factor_of * one(*cut)
    return factor_of


def scatter_about(stream_key, dims, deviation, reach, cuts=(), held_as=jnp.bfloat16):
    array = jax.random.normal(stream_key, dims, jnp.float32) * deviation
    if len(cuts) > 0:
        array = block_levels(stream_key, dims, cuts, -0.22, 0.18) * array
    return jnp.clip(array, min=-reach, max=reach).astype(held_as)


def setup_inputs(seed: int = 0) -> dict:
    keys = jax.random.split(jax.random.key(seed), 7)
    return {
        "sigma_anc": draw_sigma_anc(jax.random.fold_in(keys[6], 71), 0),
        "panels": scatter_about(keys[1], (ANCESTOR_COLUMNS, NS * NODE_WIDTH), (K1 * NODE_WIDTH) ** -0.5, 0.0625, ((0, 32),), jnp.float32),
        "diag_inv": scatter_about(keys[2], (NS * NODE_WIDTH, NODE_WIDTH), 1.0, 6.0, (), jnp.float32),
        "scaled_parent_panel": scatter_about(keys[3], (LOWER_NODES_2 * NODE_WIDTH, NODE_WIDTH), NODE_WIDTH ** -0.5, 0.375, (), jnp.float32),
        "struct_upper": draw_struct_upper(jax.random.fold_in(keys[6], 71), 0),
        "struct_lower": draw_struct_lower(jax.random.fold_in(keys[6], 71), 0),
    }


HIGH_ACCURACY = lax.Precision.HIGHEST


def block_table(struct_upper, struct_lower):
    ids = jnp.arange(NA, dtype=jnp.int32)
    upper = jnp.any(struct_upper[:, :, None] == ids[None, None, :], axis=1)
    lower = jnp.any(struct_lower[:, :, None] == ids[None, None, :], axis=1)
    return jnp.concatenate([upper, lower], axis=0).astype(jnp.float32)


def reference(sigma_anc, panels, diag_inv, scaled_parent_panel, struct_upper, struct_lower):
    table = block_table(struct_upper, struct_lower)
    rows_mask = jnp.repeat(table.T, NODE_WIDTH, axis=0)
    matrix_columns = jnp.repeat(rows_mask, NODE_WIDTH, axis=1)
    upanel = panels * matrix_columns
    inverse_complete = jnp.dot(sigma_anc, upanel, precision=HIGH_ACCURACY, preferred_element_type=jnp.float32)
    upper_width_1 = UPPER_NODES_1 * NODE_WIDTH
    g_up = -(matrix_columns[:, :upper_width_1] * inverse_complete[:, :upper_width_1])
    parent_ids = jnp.arange(LOWER_NODES_2, dtype=jnp.int32) % UPPER_NODES_1
    membership_grid = (parent_ids[:, None] == jnp.arange(UPPER_NODES_1, dtype=jnp.int32)[None, :]).astype(jnp.float32)
    collected_elder_share = jnp.einsum('rjw,cj->rcw', g_up.reshape(ANCESTOR_COLUMNS, UPPER_NODES_1, NODE_WIDTH), membership_grid, precision=HIGH_ACCURACY)
    stacked_arrays = scaled_parent_panel.reshape(LOWER_NODES_2, NODE_WIDTH, NODE_WIDTH)
    resolved_bottom_share = matrix_columns[:, upper_width_1:].reshape(ANCESTOR_COLUMNS, LOWER_NODES_2, NODE_WIDTH) * (jnp.einsum('odf,dfy->ody', collected_elder_share, stacked_arrays, precision=HIGH_ACCURACY) + inverse_complete[:, upper_width_1:].reshape(ANCESTOR_COLUMNS, LOWER_NODES_2, NODE_WIDTH))
    cov_panel = jnp.concatenate([g_up, -resolved_bottom_share.reshape(ANCESTOR_COLUMNS, LOWER_NODES_2 * NODE_WIDTH)], axis=1)
    u_up = upanel[:, :upper_width_1].reshape(ANCESTOR_COLUMNS, UPPER_NODES_1, NODE_WIDTH)
    u_low = upanel[:, upper_width_1:].reshape(ANCESTOR_COLUMNS, LOWER_NODES_2, NODE_WIDTH)
    amat = jnp.einsum('rjw,rjv->jwv', u_up, inverse_complete[:, :upper_width_1].reshape(ANCESTOR_COLUMNS, UPPER_NODES_1, NODE_WIDTH), precision=HIGH_ACCURACY)
    block_matrix = jnp.einsum('rcw,rcv->cwv', u_low, collected_elder_share, precision=HIGH_ACCURACY)
    extra_matrix = jnp.einsum('rcw,rcv->cwv', u_low, resolved_bottom_share, precision=HIGH_ACCURACY)
    diagonal_matrices = diag_inv.reshape(UPPER_NODES_1 + LOWER_NODES_2, NODE_WIDTH, NODE_WIDTH)
    s_up = diagonal_matrices[:UPPER_NODES_1] + amat
    parent_selection = jnp.einsum('cj,jwv->cwv', membership_grid, s_up, precision=HIGH_ACCURACY)
    solved_parent = jnp.einsum('ghz,gzs->ghs', parent_selection, stacked_arrays, precision=HIGH_ACCURACY) + jnp.transpose(block_matrix, (0, 2, 1))
    lower_selection = diagonal_matrices[UPPER_NODES_1:] + jnp.einsum('lmt,lmx->ltx', stacked_arrays, solved_parent, precision=HIGH_ACCURACY) + extra_matrix
    cov_diag = jnp.concatenate([s_up, lower_selection], axis=0).reshape((UPPER_NODES_1 + LOWER_NODES_2) * NODE_WIDTH, NODE_WIDTH)
    cov_parent = -solved_parent.reshape(LOWER_NODES_2 * NODE_WIDTH, NODE_WIDTH)
    return cov_panel, cov_diag, cov_parent
```

```python
import jax
import jax.numpy as jnp
from jax import lax
from jax.experimental import pallas as pl
from jax.experimental.pallas import tpu as pltpu
from jax.sharding import PartitionSpec as P

NODE_WIDTH = 256
UPPER_NODES_1 = 2
LOWER_NODES_2 = 2
F32 = jnp.float32
BF16 = jnp.bfloat16


HIGH_ACCURACY = lax.Precision.HIGHEST


CHIPS_Z, CHIPS_Y, CHIPS_X, CORES = 4, 2, 2, 2
PIECES = CHIPS_Z * CHIPS_Y * CHIPS_X * CORES
SUB = NODE_WIDTH // PIECES
SLOTS = 32
PER_STEP = 4
W = NODE_WIDTH
VMEM_BYTES = 60 * 1024 * 1024


def params(**kw):
    return pltpu.CompilerParams(vmem_limit_bytes=VMEM_BYTES, **kw)


def split(x):
    hi = x.astype(BF16)
    return hi, (x - hi.astype(F32)).astype(BF16)


def dot3(a, b):
    a_hi, a_lo = split(a)
    b_hi, b_lo = split(b)
    small = jnp.dot(a_lo, b_hi, preferred_element_type=F32) + jnp.dot(
        a_hi, b_lo, preferred_element_type=F32
    )
    return jnp.dot(a_hi, b_hi, preferred_element_type=F32) + small


def cost(flops, nbytes):
    return pl.CostEstimate(flops=flops, bytes_accessed=nbytes, transcendentals=0)


def transpose_body(x_ref, o_ref):
    for c in range(o_ref.shape[1]):
        for rb in range(2):
            t = x_ref[rb * W : (rb + 1) * W, c * W : (c + 1) * W].T
            o_ref[:, c, rb] = t.reshape(PIECES, SUB, W)


def transposed_pieces(panels, first, count):
    shape = (PIECES, count, 2, SUB, W)
    return pl.pallas_call(
        transpose_body,
        out_shape=jax.ShapeDtypeStruct(shape, F32),
        grid=(1,),
        in_specs=[pl.BlockSpec((2 * W, count * W), lambda i: (0, first // count))],
        out_specs=pl.BlockSpec(shape, lambda i: (0, 0, 0, 0, 0)),
        compiler_params=params(),
        cost_estimate=cost(0, 4 * panels.size * count // 2),
        name="transposed_pieces",
    )(panels)


def pick_body(idx_ref, a_ref, o_ref):
    for k in range(o_ref.shape[1]):
        o_ref[0, k] = a_ref[idx_ref[k]]


def picked(idx, a):
    return pl.pallas_call(
        pick_body,
        out_shape=jax.ShapeDtypeStruct((1, idx.shape[0], SUB, W), F32),
        in_specs=[
            pl.BlockSpec(memory_space=pltpu.SMEM),
            pl.BlockSpec(memory_space=pltpu.VMEM),
        ],
        out_specs=pl.BlockSpec(memory_space=pltpu.VMEM),
        compiler_params=params(),
        cost_estimate=cost(0, 4 * (a.size + idx.size * SUB * W)),
        name="picked",
    )(idx, a)


def product_body(accs, idx_ref, *refs):
    sig, lines, o_ref = refs[:PER_STEP], refs[PER_STEP:-1], refs[-1]
    step = pl.program_id(0)
    per_acc = pl.num_programs(0) // accs
    left = []
    for q in range(PER_STEP):
        left.append(jnp.concatenate([r[:, q].reshape(-1, W) for r in lines], axis=0))
    value = dot3(jnp.concatenate(left, axis=1), jnp.concatenate([r[...] for r in sig], axis=0))

    @pl.when(lax.rem(step, per_acc) == 0)
    def _():
        o_ref[0] = value

    @pl.when(lax.rem(step, per_acc) != 0)
    def _():
        o_ref[0] += value


def product(idx, sigma, pieces, accs, chunk=0):
    steps = SLOTS // PER_STEP
    cols = sigma.shape[1]
    rows = SUB * sum(p.shape[0] for p in pieces)

    def sig_spec(q):
        return pl.BlockSpec((W, cols), lambda i, idx, q=q: (idx[i * PER_STEP + q], 0))

    piece_specs = [
        pl.BlockSpec((p.shape[0], PER_STEP, SUB, W), lambda i, idx: (0, i + chunk * steps, 0, 0))
        for p in pieces
    ]
    return pl.pallas_call(
        lambda *refs: product_body(accs, *refs),
        out_shape=jax.ShapeDtypeStruct((accs, rows, cols), F32),
        grid_spec=pltpu.PrefetchScalarGridSpec(
            num_scalar_prefetch=1,
            grid=(steps,),
            in_specs=[sig_spec(q) for q in range(PER_STEP)] + piece_specs,
            out_specs=pl.BlockSpec((1, rows, cols), lambda i, idx: (lax.div(i * accs, steps), 0, 0)),
        ),
        compiler_params=params(),
        cost_estimate=cost(6 * SLOTS * rows * W * cols, 4 * SLOTS * W * (cols + rows)),
        name="product",
    )(idx, *([sigma] * PER_STEP), *pieces)


def row_flags(rows, lo, hi):
    top = lax.broadcasted_iota(jnp.int32, (rows, 1), 0) < W
    return jnp.where(top, lo.astype(F32), hi.astype(F32))


def local_lines(ref, c):
    return jnp.concatenate([ref[:, c, rb].reshape(W, W) for rb in range(2)], axis=1)


def in_order(pos_ref, zt_refs, c, scratch):
    g = 0
    for ref in zt_refs:
        for row in range(0, ref.shape[1], SUB):
            at = pl.multiple_of(pos_ref[g] * SUB, SUB)
            scratch[pl.ds(at, SUB), :] = ref[c, row : row + SUB, :]
            g += 1
    return scratch[...].T


def upper_body(flag_ref, pos_ref, zt_ref, up_ref, low_ref, diag_ref, v_ref, vt_ref, *outs):
    g_ref, gv_ref, a_ref, yp_ref, l_ref, scratch = outs
    z = in_order(pos_ref, [zt_ref], 0, scratch)
    g = -z * row_flags(z.shape[0], flag_ref[0], flag_ref[1])
    g_ref[...] = g
    on_first = flag_ref[4].astype(F32)
    a = diag_ref[0] * on_first - dot3(local_lines(up_ref, 0), g)
    a_ref[...] = a
    below = g * row_flags(z.shape[0], flag_ref[2], flag_ref[3])
    gv = dot3(below, v_ref[...])
    gv_ref[...] = gv
    u = local_lines(low_ref, 0)
    yp = dot3(a, v_ref[...]) + dot3(u, below).T
    yp_ref[...] = -yp
    l_ref[...] = dot3(vt_ref[...], yp) + dot3(u, gv) + diag_ref[1] * on_first


def upper(j, flags, pos, zt, pieces, diag, v, vt):
    cols = zt.shape[2]
    square = jax.ShapeDtypeStruct((W, W), F32)
    tall = jax.ShapeDtypeStruct((cols, W), F32)
    def whole(x):
        return pl.BlockSpec(x.shape, lambda i: (0,) * x.ndim)

    def own(s):
        return pl.BlockSpec((PIECES, 1, 2, SUB, W), lambda i: (0, s, 0, 0, 0))

    out_shape = (tall, tall, square, square, square)
    return pl.pallas_call(
        upper_body,
        out_shape=out_shape,
        grid=(1,),
        in_specs=[pl.BlockSpec(memory_space=pltpu.SMEM)] * 2
        + [whole(zt), own(j), own(UPPER_NODES_1 + j), whole(diag), whole(v), whole(vt)],
        out_specs=tuple(whole(o) for o in out_shape),
        scratch_shapes=[pltpu.VMEM((W, cols), F32)],
        compiler_params=params(),
        cost_estimate=cost(24 * W * W * (cols + W), 4 * W * (6 * cols + 8 * W)),
        name="upper",
    )(flags, pos, zt, pieces, pieces, diag, v, vt)


def lower_body(parts, flag_ref, pos_ref, *refs):
    zt_refs = refs[:parts]
    low_ref, g0, g1, gv0, gv1, l0, l1, panel_ref, late_ref, scratch = refs[parts:]
    for j, g_ref in enumerate((g0, g1)):
        panel_ref[:, j * W : (j + 1) * W] = g_ref[...]
    for c, (gv_ref, l_ref) in enumerate(((gv0, l0), (gv1, l1))):
        z = in_order(pos_ref, zt_refs, c, scratch)
        z = z * row_flags(z.shape[0], flag_ref[2 * c], flag_ref[2 * c + 1])
        col = (UPPER_NODES_1 + c) * W
        panel_ref[:, col : col + W] = -(gv_ref[...] + z)
        late_ref[c * W : (c + 1) * W, :] = l_ref[...] + dot3(local_lines(low_ref, c), z)


def lower(flags, pos, zts, low, ups):
    cols = zts[0].shape[2]
    operands = [ups[j][i] for i in (0, 1, 4) for j in range(UPPER_NODES_1)]
    def whole(x):
        return pl.BlockSpec(x.shape, lambda i: (0,) * x.ndim)

    out_shape = (
        jax.ShapeDtypeStruct((cols, 4 * W), F32),
        jax.ShapeDtypeStruct((LOWER_NODES_2 * W, W), F32),
    )
    return pl.pallas_call(
        lambda *refs: lower_body(len(zts), *refs),
        out_shape=out_shape,
        grid=(1,),
        in_specs=[pl.BlockSpec(memory_space=pltpu.SMEM)] * 2
        + [whole(z) for z in zts]
        + [pl.BlockSpec((PIECES, LOWER_NODES_2, 2, SUB, W), lambda i: (0, 1, 0, 0, 0))]
        + [whole(o) for o in operands],
        out_specs=tuple(whole(o) for o in out_shape),
        scratch_shapes=[pltpu.VMEM((W, cols), F32)],
        compiler_params=params(),
        cost_estimate=cost(12 * W * W * cols, 4 * W * (12 * cols + 6 * W)),
        name="lower",
    )(flags, pos, *zts, low, *operands)


def device_at(z, y, x, c):
    return ((z * CHIPS_Y + y) * CHIPS_X + x) * CORES + c


def moves(f):
    pairs = []
    for z in range(CHIPS_Z):
        for y in range(CHIPS_Y):
            for x in range(CHIPS_X):
                for c in range(CORES):
                    pairs.append((device_at(z, y, x, c), device_at(*f(z, y, x, c))))
    return pairs


ALONG_Z = moves(lambda z, y, x, c: ((z + 1) % CHIPS_Z, y, x, c))
AGAINST_Z = moves(lambda z, y, x, c: ((z - 1) % CHIPS_Z, y, x, c))
ALONG_Y = moves(lambda z, y, x, c: (z, 1 - y, x, c))
ALONG_X = moves(lambda z, y, x, c: (z, y, 1 - x, c))
ALONG_C = moves(lambda z, y, x, c: (z, y, x, 1 - c))


def move(x, pairs):
    return lax.ppermute(x, "blk", pairs)


def sync(values, after):
    values, after = list(values), list(after)
    anywhere = pl.BlockSpec(memory_space=pl.ANY)
    return pl.pallas_call(
        lambda *refs: None,
        out_shape=[jax.ShapeDtypeStruct(x.shape, x.dtype) for x in values],
        in_specs=[anywhere] * (len(values) + len(after)),
        out_specs=[anywhere] * len(values),
        input_output_aliases={i: i for i in range(len(values))},
        compiler_params=params(),
        cost_estimate=cost(0, 0),
        name="sync",
    )(*values, *after)


def other_core(lines):
    return [move(a, ALONG_C) for a in lines]


def piece_order(me):
    c = me % CORES
    x = me // CORES % CHIPS_X
    y = me // (CORES * CHIPS_X) % CHIPS_Y
    z = me // (CORES * CHIPS_X * CHIPS_Y)
    def chip(yy, xx, cc):
        return [
            device_at((z + CHIPS_Z - back) % CHIPS_Z, yy, xx, cc) for back in range(CHIPS_Z)
        ]

    near, corner = [], []
    for cc in (c, 1 - c):
        near.append(chip(y, x, cc) + chip(y, 1 - x, cc) + chip(1 - y, x, cc))
        corner.append(chip(1 - y, 1 - x, cc))
    return jnp.stack(near[0] + near[1] + corner[0] + corner[1]).astype(jnp.int32)


def summed(me, share):
    core = me % CORES
    kept = lax.dynamic_index_in_dim(share, core, 1, keepdims=False)
    sent = lax.dynamic_index_in_dim(share, 1 - core, 1, keepdims=False)
    half = kept + move(sent, ALONG_C)
    groups = [
        [device_at(0, 0, 0, c) + CORES * i for i in range(share.shape[0])] for c in range(CORES)
    ]
    return jnp.sum(
        lax.all_to_all(half, "blk", 0, 0, axis_index_groups=groups, tiled=True), axis=0
    )


def one_group(sigma_anc, panels, diag_inv, scaled_parent_panel, struct_upper, struct_lower):
    me = lax.axis_index("blk")
    pos = piece_order(me)
    v = scaled_parent_panel.reshape(LOWER_NODES_2, W, W)
    vt = jnp.transpose(v, (0, 2, 1))
    diag = diag_inv.reshape(UPPER_NODES_1 + LOWER_NODES_2, W, W)
    own_blocks = 2 * me + jnp.arange(2, dtype=jnp.int32)
    on_first = (me == 0).astype(jnp.int32)[None]

    def owns(row):
        return jnp.any(row[None, :] == own_blocks[:, None], axis=1).astype(jnp.int32)

    def finish_upper(j, gathered):
        zt = product(struct_upper[j], sigma_anc, gathered, 1, j)
        return upper(j, upper_flags[j], pos, zt, pieces, upper_diag[j], v[j], vt[j])

    def both_cores(lines):
        return lines + other_core(lines)

    low_blocks = struct_lower.reshape(SLOTS)
    pieces = transposed_pieces(panels, 0, 4)
    spread = lax.all_to_all(pieces, "blk", 0, 0, tiled=True).reshape(-1, SUB, W)

    def offsets(blocks, which):
        return 8 * (blocks // 2) + 2 * which + blocks % 2

    which = jnp.arange(LOWER_NODES_2, dtype=jnp.int32)[:, None]
    upper_flags = [
        jnp.concatenate([owns(struct_upper[j]), owns(struct_lower[j]), on_first])
        for j in range(UPPER_NODES_1)
    ]
    upper_diag = [jnp.stack([diag[j], diag[UPPER_NODES_1 + j]]) for j in range(UPPER_NODES_1)]
    lower_flags = jnp.concatenate([owns(struct_lower[0]), owns(struct_lower[1])])
    own = picked(offsets(struct_upper, which).reshape(-1), spread)
    own_low = picked(offsets(struct_lower, UPPER_NODES_1 + which).reshape(-1), spread)
    small = upper_flags + upper_diag + [v[0], v[1], vt[0], vt[1], lower_flags, pos, low_blocks]
    own, own_low, *small = sync([own, own_low, *small], [])
    upper_flags, upper_diag, v, vt = (small[i : i + 2] for i in range(0, 8, 2))
    lower_flags, pos, low_blocks = small[8:]

    lines, xs, ys = [own], [], []
    far_lines, far_xs, far_ys = [], [], []
    for step in range(CHIPS_Z - 1):
        moved = [move(lines[-1], d) for d in (ALONG_Z, ALONG_X, ALONG_Y)]
        swapped = [move(lines[-1], ALONG_C)]
        if step > 0:
            swapped.append(move(xs[-1] if step == 1 else ys[0], ALONG_C))
        line, x, y = sync(moved, swapped)
        lines, xs, ys = lines + [line], xs + [x], ys + [y]
        far_lines.append(swapped[0])
        if step > 0:
            (far_xs if step == 1 else far_ys).append(swapped[1])
    moved = [
        move(lines[3], ALONG_X),
        move(lines[3], ALONG_Y),
        move(ys[0], ALONG_X),
        move(xs[1], ALONG_Y),
        move(own_low, ALONG_Z),
    ]
    swapped = other_core([lines[3], xs[1], ys[1], xs[2], ys[2]])
    x3, y3, d0, d1, behind = sync(moved, swapped)
    far_lines.append(swapped[0])
    far_xs += swapped[1::2]
    far_ys += swapped[2::2]
    xs, ys = xs + [x3], ys + [y3]
    moved = [
        move(ys[2], ALONG_X),
        move(xs[3], ALONG_Y),
        move(behind, ALONG_Z),
        move(own_low, AGAINST_Z),
        jnp.concatenate([own_low, behind]),
    ]
    swapped = other_core([xs[3], ys[3], d0, d1])
    d2, d3, across, before, first_pair = sync(moved, swapped)
    far_xs.append(swapped[0])
    far_ys.append(swapped[1])
    gathered = lines + xs + ys + far_lines + far_xs + far_ys
    gathered += [d0, d1, d2, d3, swapped[2], swapped[3], *other_core([d2, d3])]

    s = [first_pair, jnp.concatenate([across, before])]
    sides = [move(a, ALONG_X) for a in s] + [move(a, ALONG_Y) for a in s]
    up0 = finish_upper(0, gathered)
    sides = list(sync(sides, [up0[2]]))
    corner = [move(sides[2], ALONG_X), move(sides[1], ALONG_Y)]
    near = both_cores(s + sides)
    up1 = finish_upper(1, gathered)
    corner = list(sync(corner, [up1[2], *near]))
    zt = product(low_blocks, sigma_anc, near + both_cores(corner), LOWER_NODES_2)
    panel, late = lower(lower_flags, pos, [zt], pieces, (up0, up1))
    chips = PIECES // CORES
    diag_share = jnp.concatenate([up0[2], up1[2], late]).reshape(chips, CORES, -1, W)
    parent_share = jnp.concatenate([up0[3], up1[3]]).reshape(chips, CORES, -1, W)
    total = summed(me, jnp.concatenate([diag_share, parent_share], axis=2))
    diag_rows = diag_share.shape[2]
    return panel, total[:diag_rows], total[diag_rows:]


def block_table(struct_upper, struct_lower, blocks):
    ids = jnp.arange(blocks, dtype=jnp.int32)
    upper = jnp.any(struct_upper[:, :, None] == ids[None, None, :], axis=1)
    lower = jnp.any(struct_lower[:, :, None] == ids[None, None, :], axis=1)
    return jnp.concatenate([upper, lower], axis=0).astype(jnp.float32)


def row_mask(table, first_row, count):
    blocks = table.shape[1]
    rows = first_row + jnp.arange(count, dtype=jnp.int32)
    membership_grid = (
        (rows // NODE_WIDTH)[:, None] == jnp.arange(blocks, dtype=jnp.int32)[None, :]
    ).astype(jnp.float32)
    return jnp.dot(
        membership_grid, table.T, precision=HIGH_ACCURACY, preferred_element_type=jnp.float32
    )


def strip_summands(reciprocal_lines, array_lines, membership_grid, stacked_arrays):
    count = reciprocal_lines.shape[0]
    upper_width_1 = UPPER_NODES_1 * NODE_WIDTH
    matrix_columns = jnp.repeat(array_lines, NODE_WIDTH, axis=1)
    g_up = -(matrix_columns[:, :upper_width_1] * reciprocal_lines[:, :upper_width_1])
    collected_elder_share = jnp.einsum(
        "rjw,cj->rcw",
        g_up.reshape(count, UPPER_NODES_1, NODE_WIDTH),
        membership_grid,
        precision=HIGH_ACCURACY,
    )
    resolved_bottom_share = matrix_columns[:, upper_width_1:].reshape(
        count, LOWER_NODES_2, NODE_WIDTH
    ) * (
        jnp.einsum("odf,dfy->ody", collected_elder_share, stacked_arrays, precision=HIGH_ACCURACY)
        + reciprocal_lines[:, upper_width_1:].reshape(count, LOWER_NODES_2, NODE_WIDTH)
    )
    strip_result = jnp.concatenate(
        [g_up, -resolved_bottom_share.reshape(count, LOWER_NODES_2 * NODE_WIDTH)], axis=1
    )
    return (strip_result, collected_elder_share, resolved_bottom_share)


def block_sums(urows, reciprocal_lines, collected_elder_share, resolved_bottom_share):
    count = urows.shape[0]
    upper_width_1 = UPPER_NODES_1 * NODE_WIDTH
    u_up = urows[:, :upper_width_1].reshape(count, UPPER_NODES_1, NODE_WIDTH)
    u_low = urows[:, upper_width_1:].reshape(count, LOWER_NODES_2, NODE_WIDTH)
    amat = jnp.einsum(
        "rjw,rjv->jwv",
        u_up,
        reciprocal_lines[:, :upper_width_1].reshape(count, UPPER_NODES_1, NODE_WIDTH),
        precision=HIGH_ACCURACY,
    )
    block_matrix = jnp.einsum("rcw,rcv->cwv", u_low, collected_elder_share, precision=HIGH_ACCURACY)
    extra_matrix = jnp.einsum("rcw,rcv->cwv", u_low, resolved_bottom_share, precision=HIGH_ACCURACY)
    return jnp.concatenate([amat, block_matrix, extra_matrix], axis=0)


def per_device(sigma_anc, panels, diag_inv, scaled_parent_panel, struct_upper, struct_lower):
    rows_grp, cols_dev = sigma_anc.shape
    rows_dev = panels.shape[0]
    grp_count = lax.axis_size("grp")
    blk_count = lax.axis_size("blk")
    grp_pos = lax.axis_index("grp")
    blk_pos = lax.axis_index("blk")
    blocks = cols_dev * blk_count // NODE_WIDTH
    table = block_table(struct_upper, struct_lower, blocks)
    parent_ids = jnp.arange(LOWER_NODES_2, dtype=jnp.int32) % UPPER_NODES_1
    membership_grid = (
        parent_ids[:, None] == jnp.arange(UPPER_NODES_1, dtype=jnp.int32)[None, :]
    ).astype(jnp.float32)
    stacked_arrays = scaled_parent_panel.reshape(LOWER_NODES_2, NODE_WIDTH, NODE_WIDTH)
    first_in = grp_pos * rows_grp + blk_pos * rows_dev
    upanel = panels * jnp.repeat(row_mask(table, first_in, rows_dev), NODE_WIDTH, axis=1)
    grouped = lax.all_gather(upanel, "blk", axis=0, tiled=True)
    partial_value = lax.dot_general(
        sigma_anc,
        grouped,
        (((0,), (0,)), ((), ())),
        precision=HIGH_ACCURACY,
        preferred_element_type=jnp.float32,
    )
    share = cols_dev // grp_count
    col_first = blk_pos * cols_dev
    root = col_first // rows_grp
    offset = jnp.clip(col_first - grp_pos * rows_grp, 0, rows_grp - cols_dev)
    own_first = col_first + grp_pos * share
    owned_mask = row_mask(table, own_first, share)
    nterms = UPPER_NODES_1 + 2 * LOWER_NODES_2
    inverse_columns = lax.psum(partial_value, "grp")
    inverse_owned = lax.dynamic_slice_in_dim(inverse_columns, grp_pos * share, share, 0)
    strip_result, collected_elder_share, resolved_bottom_share = strip_summands(
        inverse_owned, owned_mask, membership_grid, stacked_arrays
    )

    def on_root():
        u_cols = lax.dynamic_slice_in_dim(grouped, offset, cols_dev, 0)
        complete_mask = row_mask(table, col_first, cols_dev)
        discarded_result, collected_entire_factor, resolved_entire_factor = strip_summands(
            inverse_columns, complete_mask, membership_grid, stacked_arrays
        )
        return block_sums(u_cols, inverse_columns, collected_entire_factor, resolved_entire_factor)

    def off_root():
        return jnp.zeros((nterms, NODE_WIDTH, NODE_WIDTH), jnp.float32)

    terms = lax.cond(grp_pos == root, on_root, off_root)
    summed = lax.psum(terms, ("grp", "blk"))
    amat = summed[:UPPER_NODES_1]
    block_matrix = summed[UPPER_NODES_1 : UPPER_NODES_1 + LOWER_NODES_2]
    extra_matrix = summed[UPPER_NODES_1 + LOWER_NODES_2 :]
    diagonal_matrices = diag_inv.reshape(UPPER_NODES_1 + LOWER_NODES_2, NODE_WIDTH, NODE_WIDTH)
    s_up = diagonal_matrices[:UPPER_NODES_1] + amat
    parent_selection = jnp.einsum("cj,jwv->cwv", membership_grid, s_up, precision=HIGH_ACCURACY)
    solved_parent = jnp.einsum(
        "ghz,gzs->ghs", parent_selection, stacked_arrays, precision=HIGH_ACCURACY
    ) + jnp.transpose(block_matrix, (0, 2, 1))
    lower_selection = (
        diagonal_matrices[UPPER_NODES_1:]
        + jnp.einsum("lmt,lmx->ltx", stacked_arrays, solved_parent, precision=HIGH_ACCURACY)
        + extra_matrix
    )
    whole_diag = jnp.concatenate([s_up, lower_selection], axis=0).reshape(
        (UPPER_NODES_1 + LOWER_NODES_2) * NODE_WIDTH, NODE_WIDTH
    )
    whole_parent = -solved_parent.reshape(LOWER_NODES_2 * NODE_WIDTH, NODE_WIDTH)
    diag_rows = (UPPER_NODES_1 + LOWER_NODES_2) * NODE_WIDTH // blk_count
    parent_rows = LOWER_NODES_2 * NODE_WIDTH // blk_count
    cov_diag = lax.dynamic_slice_in_dim(whole_diag, blk_pos * diag_rows, diag_rows, 0)
    cov_parent = lax.dynamic_slice_in_dim(whole_parent, blk_pos * parent_rows, parent_rows, 0)
    return (strip_result, cov_diag, cov_parent)


def solution(mesh):
    single = mesh.shape["grp"] == 1 and mesh.shape["blk"] == PIECES
    return jax.shard_map(
        one_group if single else per_device,
        mesh=mesh,
        in_specs=(P("grp", "blk"), P(("grp", "blk"), None), P(), P(), P(), P()),
        out_specs=(P(("blk", "grp"), None), P("blk", None), P("blk", None)),
        check_vma=False,
    )
```

```python
import jax
import jax.numpy as jnp
from jax import lax
from jax.experimental import pallas as pl
from jax.experimental.pallas import tpu as pltpu
from jax.sharding import PartitionSpec as P

NODE_WIDTH = 256
UPPER_NODES_1 = 2
LOWER_NODES_2 = 2
F32 = jnp.float32
BF16 = jnp.bfloat16


HIGH_ACCURACY = lax.Precision.HIGHEST


CHIPS_Z, CHIPS_Y, CHIPS_X, CORES = 4, 2, 2, 2
PIECES = CHIPS_Z * CHIPS_Y * CHIPS_X * CORES
SUB = NODE_WIDTH // PIECES
SLOTS = 32
PER_STEP = 8
W = NODE_WIDTH


def params(mib):
    return pltpu.CompilerParams(vmem_limit_bytes=mib * 1024 * 1024)


def split(x):
    hi = x.astype(BF16)
    return hi, (x - hi.astype(F32)).astype(BF16)


def dot3(a, b):
    a_hi, a_lo = split(a)
    b_hi, b_lo = split(b)
    small = jnp.dot(a_lo, b_hi, preferred_element_type=F32) + jnp.dot(
        a_hi, b_lo, preferred_element_type=F32
    )
    return jnp.dot(a_hi, b_hi, preferred_element_type=F32) + small


def cost(flops, nbytes):
    return pl.CostEstimate(flops=flops, bytes_accessed=nbytes, transcendentals=0)


def transpose_body(x_ref, o_ref):
    for c in range(o_ref.shape[1]):
        for rb in range(2):
            t = x_ref[rb * W : (rb + 1) * W, c * W : (c + 1) * W].T
            o_ref[:, c, rb] = t.reshape(PIECES, SUB, W)


def transposed_pieces(panels, first, count):
    shape = (PIECES, count, 2, SUB, W)
    return pl.pallas_call(
        transpose_body,
        out_shape=jax.ShapeDtypeStruct(shape, F32),
        grid=(1,),
        in_specs=[pl.BlockSpec((2 * W, count * W), lambda i: (0, first // count))],
        out_specs=pl.BlockSpec(shape, lambda i: (0, 0, 0, 0, 0)),
        compiler_params=params(16),
        cost_estimate=cost(0, 4 * panels.size * count // 2),
        name="transposed_pieces",
    )(panels)


def pick_body(idx_ref, a_ref, o_ref):
    for k in range(o_ref.shape[1]):
        o_ref[0, k] = a_ref[idx_ref[k]]


def picked(idx, a):
    return pl.pallas_call(
        pick_body,
        out_shape=jax.ShapeDtypeStruct((1, idx.shape[0], SUB, W), F32),
        in_specs=[
            pl.BlockSpec(memory_space=pltpu.SMEM),
            pl.BlockSpec(memory_space=pltpu.VMEM),
        ],
        out_specs=pl.BlockSpec(memory_space=pltpu.VMEM),
        compiler_params=params(16),
        cost_estimate=cost(0, 4 * (a.size + idx.size * SUB * W)),
        name="picked",
    )(idx, a)


def product_body(accs, idx_ref, *refs):
    sig, lines, o_ref = refs[:PER_STEP], refs[PER_STEP:-1], refs[-1]
    step = pl.program_id(0)
    per_acc = pl.num_programs(0) // accs
    left = []
    for q in range(PER_STEP):
        left.append(jnp.concatenate([r[:, q].reshape(-1, W) for r in lines], axis=0))
    value = dot3(jnp.concatenate(left, axis=1), jnp.concatenate([r[...] for r in sig], axis=0))

    @pl.when(lax.rem(step, per_acc) == 0)
    def _():
        o_ref[0] = value

    @pl.when(lax.rem(step, per_acc) != 0)
    def _():
        o_ref[0] += value


def product(idx, sigma, pieces, accs, chunk=0, mib=40):
    steps = SLOTS // PER_STEP
    cols = sigma.shape[1]
    rows = SUB * sum(p.shape[0] for p in pieces)

    def sig_spec(q):
        return pl.BlockSpec((W, cols), lambda i, idx, q=q: (idx[i * PER_STEP + q], 0))

    piece_specs = [
        pl.BlockSpec((p.shape[0], PER_STEP, SUB, W), lambda i, idx: (0, i + chunk * steps, 0, 0))
        for p in pieces
    ]
    return pl.pallas_call(
        lambda *refs: product_body(accs, *refs),
        out_shape=jax.ShapeDtypeStruct((accs, rows, cols), F32),
        grid_spec=pltpu.PrefetchScalarGridSpec(
            num_scalar_prefetch=1,
            grid=(steps,),
            in_specs=[sig_spec(q) for q in range(PER_STEP)] + piece_specs,
            out_specs=pl.BlockSpec((1, rows, cols), lambda i, idx: (lax.div(i * accs, steps), 0, 0)),
        ),
        compiler_params=params(mib),
        cost_estimate=cost(6 * SLOTS * rows * W * cols, 4 * SLOTS * W * (cols + rows)),
        name="product",
    )(idx, *([sigma] * PER_STEP), *pieces)


def row_flags(rows, lo, hi):
    top = lax.broadcasted_iota(jnp.int32, (rows, 1), 0) < W
    return jnp.where(top, lo.astype(F32), hi.astype(F32))


def local_lines(ref, c):
    return jnp.concatenate([ref[:, c, rb].reshape(W, W) for rb in range(2)], axis=1)


def in_order(pos_ref, zt_refs, c, scratch):
    g = 0
    for ref in zt_refs:
        for row in range(0, ref.shape[1], SUB):
            at = pl.multiple_of(pos_ref[g] * SUB, SUB)
            scratch[pl.ds(at, SUB), :] = ref[c, row : row + SUB, :]
            g += 1
    return scratch[...].T


def upper_body(flag_ref, pos_ref, zt_ref, up_ref, low_ref, diag_ref, v_ref, vt_ref, *outs):
    g_ref, gv_ref, a_ref, yp_ref, l_ref, scratch = outs
    z = in_order(pos_ref, [zt_ref], 0, scratch)
    g = -z * row_flags(z.shape[0], flag_ref[0], flag_ref[1])
    g_ref[...] = g
    on_first = flag_ref[4].astype(F32)
    a = diag_ref[0] * on_first - dot3(local_lines(up_ref, 0), g)
    a_ref[...] = a
    below = g * row_flags(z.shape[0], flag_ref[2], flag_ref[3])
    gv = dot3(below, v_ref[...])
    gv_ref[...] = gv
    u = local_lines(low_ref, 0)
    yp = dot3(a, v_ref[...]) + dot3(u, below).T
    yp_ref[...] = -yp
    l_ref[...] = dot3(vt_ref[...], yp) + dot3(u, gv) + diag_ref[1] * on_first


def upper(j, flags, pos, zt, pieces, diag, v, vt):
    cols = zt.shape[2]
    square = jax.ShapeDtypeStruct((W, W), F32)
    tall = jax.ShapeDtypeStruct((cols, W), F32)
    def whole(x):
        return pl.BlockSpec(x.shape, lambda i: (0,) * x.ndim)

    def own(s):
        return pl.BlockSpec((PIECES, 1, 2, SUB, W), lambda i: (0, s, 0, 0, 0))

    out_shape = (tall, tall, square, square, square)
    return pl.pallas_call(
        upper_body,
        out_shape=out_shape,
        grid=(1,),
        in_specs=[pl.BlockSpec(memory_space=pltpu.SMEM)] * 2
        + [whole(zt), own(j), own(UPPER_NODES_1 + j), whole(diag), whole(v), whole(vt)],
        out_specs=tuple(whole(o) for o in out_shape),
        scratch_shapes=[pltpu.VMEM((W, cols), F32)],
        compiler_params=params(24),
        cost_estimate=cost(24 * W * W * (cols + W), 4 * W * (6 * cols + 8 * W)),
        name="upper",
    )(flags, pos, zt, pieces, pieces, diag, v, vt)


def lower_body(parts, flag_ref, pos_ref, *refs):
    zt_refs = refs[:parts]
    low_ref, g0, g1, gv0, gv1, l0, l1, panel_ref, late_ref, scratch = refs[parts:]
    for j, g_ref in enumerate((g0, g1)):
        panel_ref[:, j * W : (j + 1) * W] = g_ref[...]
    for c, (gv_ref, l_ref) in enumerate(((gv0, l0), (gv1, l1))):
        z = in_order(pos_ref, zt_refs, c, scratch)
        z = z * row_flags(z.shape[0], flag_ref[2 * c], flag_ref[2 * c + 1])
        col = (UPPER_NODES_1 + c) * W
        panel_ref[:, col : col + W] = -(gv_ref[...] + z)
        late_ref[c * W : (c + 1) * W, :] = l_ref[...] + dot3(local_lines(low_ref, c), z)


def lower(flags, pos, zts, low, ups):
    cols = zts[0].shape[2]
    operands = [ups[j][i] for i in (0, 1, 4) for j in range(UPPER_NODES_1)]
    def whole(x):
        return pl.BlockSpec(x.shape, lambda i: (0,) * x.ndim)

    out_shape = (
        jax.ShapeDtypeStruct((cols, 4 * W), F32),
        jax.ShapeDtypeStruct((LOWER_NODES_2 * W, W), F32),
    )
    return pl.pallas_call(
        lambda *refs: lower_body(len(zts), *refs),
        out_shape=out_shape,
        grid=(1,),
        in_specs=[pl.BlockSpec(memory_space=pltpu.SMEM)] * 2
        + [whole(z) for z in zts]
        + [pl.BlockSpec((PIECES, LOWER_NODES_2, 2, SUB, W), lambda i: (0, 1, 0, 0, 0))]
        + [whole(o) for o in operands],
        out_specs=tuple(whole(o) for o in out_shape),
        scratch_shapes=[pltpu.VMEM((W, cols), F32)],
        compiler_params=params(32),
        cost_estimate=cost(12 * W * W * cols, 4 * W * (12 * cols + 6 * W)),
        name="lower",
    )(flags, pos, *zts, low, *operands)


def device_at(z, y, x, c):
    return ((z * CHIPS_Y + y) * CHIPS_X + x) * CORES + c


def moves(f):
    pairs = []
    for z in range(CHIPS_Z):
        for y in range(CHIPS_Y):
            for x in range(CHIPS_X):
                for c in range(CORES):
                    pairs.append((device_at(z, y, x, c), device_at(*f(z, y, x, c))))
    return pairs


ALONG_Z = moves(lambda z, y, x, c: ((z + 1) % CHIPS_Z, y, x, c))
AGAINST_Z = moves(lambda z, y, x, c: ((z - 1) % CHIPS_Z, y, x, c))
ALONG_Y = moves(lambda z, y, x, c: (z, 1 - y, x, c))
ALONG_X = moves(lambda z, y, x, c: (z, y, 1 - x, c))
ALONG_C = moves(lambda z, y, x, c: (z, y, x, 1 - c))


def move(x, pairs):
    return lax.ppermute(x, "blk", pairs)


def sync(values, after):
    values, after = list(values), list(after)
    anywhere = pl.BlockSpec(memory_space=pl.ANY)
    return pl.pallas_call(
        lambda *refs: None,
        out_shape=[jax.ShapeDtypeStruct(x.shape, x.dtype) for x in values],
        in_specs=[anywhere] * (len(values) + len(after)),
        out_specs=[anywhere] * len(values),
        input_output_aliases={i: i for i in range(len(values))},
        compiler_params=params(1),
        cost_estimate=cost(0, 0),
        name="sync",
    )(*values, *after)


def other_core(lines):
    return [move(a, ALONG_C) for a in lines]


def piece_order(me):
    c = me % CORES
    x = me // CORES % CHIPS_X
    y = me // (CORES * CHIPS_X) % CHIPS_Y
    z = me // (CORES * CHIPS_X * CHIPS_Y)
    def chip(yy, xx, cc):
        return [
            device_at((z + CHIPS_Z - back) % CHIPS_Z, yy, xx, cc) for back in range(CHIPS_Z)
        ]

    near, corner = [], []
    for cc in (c, 1 - c):
        near.append(chip(y, x, cc) + chip(y, 1 - x, cc) + chip(1 - y, x, cc))
        corner.append(chip(1 - y, 1 - x, cc))
    return jnp.stack(near[0] + near[1] + corner[0] + corner[1]).astype(jnp.int32)


def exchanged(x, groups):
    return lax.all_to_all(x, "blk", 0, 0, axis_index_groups=groups, tiled=True)


def summed(me, share):
    core = me % CORES
    kept = lax.dynamic_index_in_dim(share, core, 2, keepdims=False)
    sent = lax.dynamic_index_in_dim(share, 1 - core, 2, keepdims=False)
    plane = [device_at(0, y, x, 0) for y in range(CHIPS_Y) for x in range(CHIPS_X)]
    column = [device_at(z, 0, 0, 0) for z in range(CHIPS_Z)]
    total = kept + move(sent, ALONG_C)
    total = exchanged(total, [[p + q + c for p in plane] for q in column for c in range(CORES)])
    total = jnp.sum(total, axis=0)
    total = exchanged(total, [[p + q + c for q in column] for p in plane for c in range(CORES)])
    return jnp.sum(total, axis=0)


def one_group(sigma_anc, panels, diag_inv, scaled_parent_panel, struct_upper, struct_lower):
    me = lax.axis_index("blk")
    pos = piece_order(me)
    v = scaled_parent_panel.reshape(LOWER_NODES_2, W, W)
    vt = jnp.transpose(v, (0, 2, 1))
    diag = diag_inv.reshape(UPPER_NODES_1 + LOWER_NODES_2, W, W)
    own_blocks = 2 * me + jnp.arange(2, dtype=jnp.int32)
    on_first = (me == 0).astype(jnp.int32)[None]

    def owns(row):
        return jnp.any(row[None, :] == own_blocks[:, None], axis=1).astype(jnp.int32)

    def finish_upper(j, gathered):
        zt = product(struct_upper[j], sigma_anc, gathered, 1, j)
        return upper(j, upper_flags[j], pos, zt, pieces, upper_diag[j], v[j], vt[j])

    def both_cores(lines):
        return lines + other_core(lines)

    low_blocks = struct_lower.reshape(SLOTS)
    pieces = transposed_pieces(panels, 0, 4)
    spread = lax.all_to_all(pieces, "blk", 0, 0, tiled=True).reshape(-1, SUB, W)

    def offsets(blocks, which):
        return 8 * (blocks // 2) + 2 * which + blocks % 2

    which = jnp.arange(LOWER_NODES_2, dtype=jnp.int32)[:, None]
    upper_flags = [
        jnp.concatenate([owns(struct_upper[j]), owns(struct_lower[j]), on_first])
        for j in range(UPPER_NODES_1)
    ]
    upper_diag = [jnp.stack([diag[j], diag[UPPER_NODES_1 + j]]) for j in range(UPPER_NODES_1)]
    lower_flags = jnp.concatenate([owns(struct_lower[0]), owns(struct_lower[1])])
    own = picked(offsets(struct_upper, which).reshape(-1), spread)
    own_low = picked(offsets(struct_lower, UPPER_NODES_1 + which).reshape(-1), spread)
    small = upper_flags + upper_diag + [v[0], v[1], vt[0], vt[1], lower_flags, pos, low_blocks]
    (own,) = sync([own], small)
    v, vt = small[4:6], small[6:8]

    lines, xs, ys = [own], [], []
    far_lines, far_xs, far_ys = [], [], []
    for step in range(CHIPS_Z - 1):
        moved = [move(lines[-1], d) for d in (ALONG_Z, ALONG_X, ALONG_Y)]
        swapped = [move(lines[-1], ALONG_C)]
        if step > 0:
            swapped.append(move(xs[-1] if step == 1 else ys[0], ALONG_C))
        if step == 0:
            line, x, y, own_low = sync(moved + [own_low], swapped)
        else:
            line, x, y = sync(moved, swapped)
        lines, xs, ys = lines + [line], xs + [x], ys + [y]
        far_lines.append(swapped[0])
        if step > 0:
            (far_xs if step == 1 else far_ys).append(swapped[1])
    moved = [
        move(lines[3], ALONG_X),
        move(lines[3], ALONG_Y),
        move(ys[0], ALONG_X),
        move(xs[1], ALONG_Y),
        move(own_low, ALONG_Z),
    ]
    swapped = other_core([lines[3], xs[1], ys[1], xs[2], ys[2]])
    x3, y3, d0, d1, behind = sync(moved, swapped)
    far_lines.append(swapped[0])
    far_xs += swapped[1::2]
    far_ys += swapped[2::2]
    xs, ys = xs + [x3], ys + [y3]
    moved = [
        move(ys[2], ALONG_X),
        move(xs[3], ALONG_Y),
        move(behind, ALONG_Z),
        move(own_low, AGAINST_Z),
        jnp.concatenate([own_low, behind]),
    ]
    swapped = other_core([xs[3], ys[3], d0, d1])
    d2, d3, across, before, first_pair = sync(moved, swapped)
    far_xs.append(swapped[0])
    far_ys.append(swapped[1])
    gathered = lines + xs + ys + far_lines + far_xs + far_ys
    gathered += [d0, d1, d2, d3, swapped[2], swapped[3], *other_core([d2, d3])]

    s = [first_pair, jnp.concatenate([across, before])]
    sides = [move(a, ALONG_X) for a in s] + [move(a, ALONG_Y) for a in s]
    up0 = finish_upper(0, gathered)
    sides = list(sync(sides, [up0[2]]))
    corner = [move(sides[2], ALONG_X), move(sides[1], ALONG_Y)]
    near = both_cores(s + sides)
    up1 = finish_upper(1, gathered)
    corner = list(sync(corner, [up1[2], *near]))
    zt = product(low_blocks, sigma_anc, near + both_cores(corner), LOWER_NODES_2, mib=60)
    panel, late = lower(lower_flags, pos, [zt], pieces, (up0, up1))
    by_device = (CHIPS_Z, CHIPS_Y * CHIPS_X, CORES, -1, W)
    diag_share = jnp.concatenate([up0[2], up1[2], late]).reshape(by_device)
    parent_share = jnp.concatenate([up0[3], up1[3]]).reshape(by_device)
    total = summed(me, jnp.swapaxes(jnp.concatenate([diag_share, parent_share], axis=3), 0, 1))
    diag_rows = diag_share.shape[3]
    return panel, total[:diag_rows], total[diag_rows:]


def block_table(struct_upper, struct_lower, blocks):
    ids = jnp.arange(blocks, dtype=jnp.int32)
    upper = jnp.any(struct_upper[:, :, None] == ids[None, None, :], axis=1)
    lower = jnp.any(struct_lower[:, :, None] == ids[None, None, :], axis=1)
    return jnp.concatenate([upper, lower], axis=0).astype(jnp.float32)


def row_mask(table, first_row, count):
    blocks = table.shape[1]
    rows = first_row + jnp.arange(count, dtype=jnp.int32)
    membership_grid = (
        (rows // NODE_WIDTH)[:, None] == jnp.arange(blocks, dtype=jnp.int32)[None, :]
    ).astype(jnp.float32)
    return jnp.dot(
        membership_grid, table.T, precision=HIGH_ACCURACY, preferred_element_type=jnp.float32
    )


def strip_summands(reciprocal_lines, array_lines, membership_grid, stacked_arrays):
    count = reciprocal_lines.shape[0]
    upper_width_1 = UPPER_NODES_1 * NODE_WIDTH
    matrix_columns = jnp.repeat(array_lines, NODE_WIDTH, axis=1)
    g_up = -(matrix_columns[:, :upper_width_1] * reciprocal_lines[:, :upper_width_1])
    collected_elder_share = jnp.einsum(
        "rjw,cj->rcw",
        g_up.reshape(count, UPPER_NODES_1, NODE_WIDTH),
        membership_grid,
        precision=HIGH_ACCURACY,
    )
    resolved_bottom_share = matrix_columns[:, upper_width_1:].reshape(
        count, LOWER_NODES_2, NODE_WIDTH
    ) * (
        jnp.einsum("odf,dfy->ody", collected_elder_share, stacked_arrays, precision=HIGH_ACCURACY)
        + reciprocal_lines[:, upper_width_1:].reshape(count, LOWER_NODES_2, NODE_WIDTH)
    )
    strip_result = jnp.concatenate(
        [g_up, -resolved_bottom_share.reshape(count, LOWER_NODES_2 * NODE_WIDTH)], axis=1
    )
    return (strip_result, collected_elder_share, resolved_bottom_share)


def block_sums(urows, reciprocal_lines, collected_elder_share, resolved_bottom_share):
    count = urows.shape[0]
    upper_width_1 = UPPER_NODES_1 * NODE_WIDTH
    u_up = urows[:, :upper_width_1].reshape(count, UPPER_NODES_1, NODE_WIDTH)
    u_low = urows[:, upper_width_1:].reshape(count, LOWER_NODES_2, NODE_WIDTH)
    amat = jnp.einsum(
        "rjw,rjv->jwv",
        u_up,
        reciprocal_lines[:, :upper_width_1].reshape(count, UPPER_NODES_1, NODE_WIDTH),
        precision=HIGH_ACCURACY,
    )
    block_matrix = jnp.einsum("rcw,rcv->cwv", u_low, collected_elder_share, precision=HIGH_ACCURACY)
    extra_matrix = jnp.einsum("rcw,rcv->cwv", u_low, resolved_bottom_share, precision=HIGH_ACCURACY)
    return jnp.concatenate([amat, block_matrix, extra_matrix], axis=0)


def per_device(sigma_anc, panels, diag_inv, scaled_parent_panel, struct_upper, struct_lower):
    rows_grp, cols_dev = sigma_anc.shape
    rows_dev = panels.shape[0]
    grp_count = lax.axis_size("grp")
    blk_count = lax.axis_size("blk")
    grp_pos = lax.axis_index("grp")
    blk_pos = lax.axis_index("blk")
    blocks = cols_dev * blk_count // NODE_WIDTH
    table = block_table(struct_upper, struct_lower, blocks)
    parent_ids = jnp.arange(LOWER_NODES_2, dtype=jnp.int32) % UPPER_NODES_1
    membership_grid = (
        parent_ids[:, None] == jnp.arange(UPPER_NODES_1, dtype=jnp.int32)[None, :]
    ).astype(jnp.float32)
    stacked_arrays = scaled_parent_panel.reshape(LOWER_NODES_2, NODE_WIDTH, NODE_WIDTH)
    first_in = grp_pos * rows_grp + blk_pos * rows_dev
    upanel = panels * jnp.repeat(row_mask(table, first_in, rows_dev), NODE_WIDTH, axis=1)
    grouped = lax.all_gather(upanel, "blk", axis=0, tiled=True)
    partial_value = lax.dot_general(
        sigma_anc,
        grouped,
        (((0,), (0,)), ((), ())),
        precision=HIGH_ACCURACY,
        preferred_element_type=jnp.float32,
    )
    share = cols_dev // grp_count
    col_first = blk_pos * cols_dev
    root = col_first // rows_grp
    offset = jnp.clip(col_first - grp_pos * rows_grp, 0, rows_grp - cols_dev)
    own_first = col_first + grp_pos * share
    owned_mask = row_mask(table, own_first, share)
    nterms = UPPER_NODES_1 + 2 * LOWER_NODES_2
    inverse_columns = lax.psum(partial_value, "grp")
    inverse_owned = lax.dynamic_slice_in_dim(inverse_columns, grp_pos * share, share, 0)
    strip_result, collected_elder_share, resolved_bottom_share = strip_summands(
        inverse_owned, owned_mask, membership_grid, stacked_arrays
    )

    def on_root():
        u_cols = lax.dynamic_slice_in_dim(grouped, offset, cols_dev, 0)
        complete_mask = row_mask(table, col_first, cols_dev)
        discarded_result, collected_entire_factor, resolved_entire_factor = strip_summands(
            inverse_columns, complete_mask, membership_grid, stacked_arrays
        )
        return block_sums(u_cols, inverse_columns, collected_entire_factor, resolved_entire_factor)

    def off_root():
        return jnp.zeros((nterms, NODE_WIDTH, NODE_WIDTH), jnp.float32)

    terms = lax.cond(grp_pos == root, on_root, off_root)
    summed = lax.psum(terms, ("grp", "blk"))
    amat = summed[:UPPER_NODES_1]
    block_matrix = summed[UPPER_NODES_1 : UPPER_NODES_1 + LOWER_NODES_2]
    extra_matrix = summed[UPPER_NODES_1 + LOWER_NODES_2 :]
    diagonal_matrices = diag_inv.reshape(UPPER_NODES_1 + LOWER_NODES_2, NODE_WIDTH, NODE_WIDTH)
    s_up = diagonal_matrices[:UPPER_NODES_1] + amat
    parent_selection = jnp.einsum("cj,jwv->cwv", membership_grid, s_up, precision=HIGH_ACCURACY)
    solved_parent = jnp.einsum(
        "ghz,gzs->ghs", parent_selection, stacked_arrays, precision=HIGH_ACCURACY
    ) + jnp.transpose(block_matrix, (0, 2, 1))
    lower_selection = (
        diagonal_matrices[UPPER_NODES_1:]
        + jnp.einsum("lmt,lmx->ltx", stacked_arrays, solved_parent, precision=HIGH_ACCURACY)
        + extra_matrix
    )
    whole_diag = jnp.concatenate([s_up, lower_selection], axis=0).reshape(
        (UPPER_NODES_1 + LOWER_NODES_2) * NODE_WIDTH, NODE_WIDTH
    )
    whole_parent = -solved_parent.reshape(LOWER_NODES_2 * NODE_WIDTH, NODE_WIDTH)
    diag_rows = (UPPER_NODES_1 + LOWER_NODES_2) * NODE_WIDTH // blk_count
    parent_rows = LOWER_NODES_2 * NODE_WIDTH // blk_count
    cov_diag = lax.dynamic_slice_in_dim(whole_diag, blk_pos * diag_rows, diag_rows, 0)
    cov_parent = lax.dynamic_slice_in_dim(whole_parent, blk_pos * parent_rows, parent_rows, 0)
    return (strip_result, cov_diag, cov_parent)


def solution(mesh):
    single = mesh.shape["grp"] == 1 and mesh.shape["blk"] == PIECES
    return jax.shard_map(
        one_group if single else per_device,
        mesh=mesh,
        in_specs=(P("grp", "blk"), P(("grp", "blk"), None), P(), P(), P(), P()),
        out_specs=(P(("blk", "grp"), None), P("blk", None), P("blk", None)),
        check_vma=False,
    )
```

```python
import jax
import jax.numpy as jnp
from jax import lax
from jax.experimental import pallas as pl
from jax.experimental.pallas import tpu as pltpu
from jax.sharding import PartitionSpec as P

NODE_WIDTH = 256
UPPER_NODES_1 = 2
LOWER_NODES_2 = 2
F32 = jnp.float32
BF16 = jnp.bfloat16


HIGH_ACCURACY = lax.Precision.HIGHEST


CHIPS_Z, CHIPS_Y, CHIPS_X, CORES = 4, 2, 2, 2
PIECES = CHIPS_Z * CHIPS_Y * CHIPS_X * CORES
SUB = NODE_WIDTH // PIECES
SLOTS = 32
PER_STEP = 4
W = NODE_WIDTH


def params(mib):
    return pltpu.CompilerParams(vmem_limit_bytes=mib * 1024 * 1024)


def split(x):
    hi = x.astype(BF16)
    return hi, (x - hi.astype(F32)).astype(BF16)


def dot3(a, b):
    a_hi, a_lo = split(a)
    b_hi, b_lo = split(b)
    small = jnp.dot(a_lo, b_hi, preferred_element_type=F32) + jnp.dot(
        a_hi, b_lo, preferred_element_type=F32
    )
    return jnp.dot(a_hi, b_hi, preferred_element_type=F32) + small


def cost(flops, nbytes):
    return pl.CostEstimate(flops=flops, bytes_accessed=nbytes, transcendentals=0)


def transpose_body(x_ref, o_ref):
    for c in range(o_ref.shape[1]):
        for rb in range(2):
            t = x_ref[rb * W : (rb + 1) * W, c * W : (c + 1) * W].T
            o_ref[:, c, rb] = t.reshape(PIECES, SUB, W)


def transposed_pieces(panels, first, count):
    shape = (PIECES, count, 2, SUB, W)
    return pl.pallas_call(
        transpose_body,
        out_shape=jax.ShapeDtypeStruct(shape, F32),
        grid=(1,),
        in_specs=[pl.BlockSpec((2 * W, count * W), lambda i: (0, first // count))],
        out_specs=pl.BlockSpec(shape, lambda i: (0, 0, 0, 0, 0)),
        compiler_params=params(16),
        cost_estimate=cost(0, 4 * panels.size * count // 2),
        name="transposed_pieces",
    )(panels)


def pick_body(idx_ref, a_ref, o_ref):
    for k in range(o_ref.shape[1]):
        o_ref[0, k] = a_ref[idx_ref[k]]


def picked(idx, a):
    return pl.pallas_call(
        pick_body,
        out_shape=jax.ShapeDtypeStruct((1, idx.shape[0], SUB, W), F32),
        in_specs=[
            pl.BlockSpec(memory_space=pltpu.SMEM),
            pl.BlockSpec(memory_space=pltpu.VMEM),
        ],
        out_specs=pl.BlockSpec(memory_space=pltpu.VMEM),
        compiler_params=params(16),
        cost_estimate=cost(0, 4 * (a.size + idx.size * SUB * W)),
        name="picked",
    )(idx, a)


def product_body(accs, idx_ref, *refs):
    sig, lines, o_ref = refs[:PER_STEP], refs[PER_STEP:-1], refs[-1]
    step = pl.program_id(0)
    per_acc = pl.num_programs(0) // accs
    left = []
    for q in range(PER_STEP):
        left.append(jnp.concatenate([r[:, q].reshape(-1, W) for r in lines], axis=0))
    value = dot3(jnp.concatenate(left, axis=1), jnp.concatenate([r[...] for r in sig], axis=0))

    @pl.when(lax.rem(step, per_acc) == 0)
    def _():
        o_ref[0] = value

    @pl.when(lax.rem(step, per_acc) != 0)
    def _():
        o_ref[0] += value


def product(idx, sigma, pieces, accs, chunk=0, mib=18):
    steps = SLOTS // PER_STEP
    cols = sigma.shape[1]
    rows = SUB * sum(p.shape[0] for p in pieces)

    def sig_spec(q):
        return pl.BlockSpec((W, cols), lambda i, idx, q=q: (idx[i * PER_STEP + q], 0))

    piece_specs = [
        pl.BlockSpec((p.shape[0], PER_STEP, SUB, W), lambda i, idx: (0, i + chunk * steps, 0, 0))
        for p in pieces
    ]
    return pl.pallas_call(
        lambda *refs: product_body(accs, *refs),
        out_shape=jax.ShapeDtypeStruct((accs, rows, cols), F32),
        grid_spec=pltpu.PrefetchScalarGridSpec(
            num_scalar_prefetch=1,
            grid=(steps,),
            in_specs=[sig_spec(q) for q in range(PER_STEP)] + piece_specs,
            out_specs=pl.BlockSpec((1, rows, cols), lambda i, idx: (lax.div(i * accs, steps), 0, 0)),
        ),
        compiler_params=params(mib),
        cost_estimate=cost(6 * SLOTS * rows * W * cols, 4 * SLOTS * W * (cols + rows)),
        name="product",
    )(idx, *([sigma] * PER_STEP), *pieces)


def row_flags(rows, lo, hi):
    top = lax.broadcasted_iota(jnp.int32, (rows, 1), 0) < W
    return jnp.where(top, lo.astype(F32), hi.astype(F32))


def local_lines(ref, c):
    return jnp.concatenate([ref[:, c, rb].reshape(W, W) for rb in range(2)], axis=1)


def in_order(pos_ref, zt_refs, c, scratch):
    g = 0
    for ref in zt_refs:
        for row in range(0, ref.shape[1], SUB):
            at = pl.multiple_of(pos_ref[g] * SUB, SUB)
            scratch[pl.ds(at, SUB), :] = ref[c, row : row + SUB, :]
            g += 1
    return scratch[...].T


def upper_body(flag_ref, pos_ref, zt_ref, up_ref, low_ref, diag_ref, v_ref, vt_ref, *outs):
    g_ref, gv_ref, a_ref, yp_ref, l_ref, scratch = outs
    z = in_order(pos_ref, [zt_ref], 0, scratch)
    g = -z * row_flags(z.shape[0], flag_ref[0], flag_ref[1])
    g_ref[...] = g
    on_first = flag_ref[4].astype(F32)
    a = diag_ref[0] * on_first - dot3(local_lines(up_ref, 0), g)
    a_ref[...] = a
    below = g * row_flags(z.shape[0], flag_ref[2], flag_ref[3])
    gv = dot3(below, v_ref[...])
    gv_ref[...] = gv
    u = local_lines(low_ref, 0)
    yp = dot3(a, v_ref[...]) + dot3(u, below).T
    yp_ref[...] = -yp
    l_ref[...] = dot3(vt_ref[...], yp) + dot3(u, gv) + diag_ref[1] * on_first


def upper(j, flags, pos, zt, pieces, diag, v, vt):
    cols = zt.shape[2]
    square = jax.ShapeDtypeStruct((W, W), F32)
    tall = jax.ShapeDtypeStruct((cols, W), F32)
    def whole(x):
        return pl.BlockSpec(x.shape, lambda i: (0,) * x.ndim)

    def own(s):
        return pl.BlockSpec((PIECES, 1, 2, SUB, W), lambda i: (0, s, 0, 0, 0))

    out_shape = (tall, tall, square, square, square)
    return pl.pallas_call(
        upper_body,
        out_shape=out_shape,
        grid=(1,),
        in_specs=[pl.BlockSpec(memory_space=pltpu.SMEM)] * 2
        + [whole(zt), own(j), own(UPPER_NODES_1 + j), whole(diag), whole(v), whole(vt)],
        out_specs=tuple(whole(o) for o in out_shape),
        scratch_shapes=[pltpu.VMEM((W, cols), F32)],
        compiler_params=params(24),
        cost_estimate=cost(24 * W * W * (cols + W), 4 * W * (6 * cols + 8 * W)),
        name="upper",
    )(flags, pos, zt, pieces, pieces, diag, v, vt)


def lower_body(parts, flag_ref, pos_ref, *refs):
    zt_refs = refs[:parts]
    low_ref, g0, g1, gv0, gv1, l0, l1, panel_ref, late_ref, scratch = refs[parts:]
    for j, g_ref in enumerate((g0, g1)):
        panel_ref[:, j * W : (j + 1) * W] = g_ref[...]
    for c, (gv_ref, l_ref) in enumerate(((gv0, l0), (gv1, l1))):
        z = in_order(pos_ref, zt_refs, c, scratch)
        z = z * row_flags(z.shape[0], flag_ref[2 * c], flag_ref[2 * c + 1])
        col = (UPPER_NODES_1 + c) * W
        panel_ref[:, col : col + W] = -(gv_ref[...] + z)
        late_ref[c * W : (c + 1) * W, :] = l_ref[...] + dot3(local_lines(low_ref, c), z)


def lower(flags, pos, zts, low, ups):
    cols = zts[0].shape[2]
    operands = [ups[j][i] for i in (0, 1, 4) for j in range(UPPER_NODES_1)]
    def whole(x):
        return pl.BlockSpec(x.shape, lambda i: (0,) * x.ndim)

    out_shape = (
        jax.ShapeDtypeStruct((cols, 4 * W), F32),
        jax.ShapeDtypeStruct((LOWER_NODES_2 * W, W), F32),
    )
    return pl.pallas_call(
        lambda *refs: lower_body(len(zts), *refs),
        out_shape=out_shape,
        grid=(1,),
        in_specs=[pl.BlockSpec(memory_space=pltpu.SMEM)] * 2
        + [whole(z) for z in zts]
        + [pl.BlockSpec((PIECES, LOWER_NODES_2, 2, SUB, W), lambda i: (0, 1, 0, 0, 0))]
        + [whole(o) for o in operands],
        out_specs=tuple(whole(o) for o in out_shape),
        scratch_shapes=[pltpu.VMEM((W, cols), F32)],
        compiler_params=params(32),
        cost_estimate=cost(12 * W * W * cols, 4 * W * (12 * cols + 6 * W)),
        name="lower",
    )(flags, pos, *zts, low, *operands)


def device_at(z, y, x, c):
    return ((z * CHIPS_Y + y) * CHIPS_X + x) * CORES + c


def moves(f):
    pairs = []
    for z in range(CHIPS_Z):
        for y in range(CHIPS_Y):
            for x in range(CHIPS_X):
                for c in range(CORES):
                    pairs.append((device_at(z, y, x, c), device_at(*f(z, y, x, c))))
    return pairs


ALONG_Z = moves(lambda z, y, x, c: ((z + 1) % CHIPS_Z, y, x, c))
AGAINST_Z = moves(lambda z, y, x, c: ((z - 1) % CHIPS_Z, y, x, c))
DIAGONAL = moves(lambda z, y, x, c: (z, 1 - y, 1 - x, c))
Z_BY = [moves(lambda z, y, x, c, s=s: ((z + s) % CHIPS_Z, y, x, c)) for s in range(CHIPS_Z)]
ALONG_Y = moves(lambda z, y, x, c: (z, 1 - y, x, c))
ALONG_X = moves(lambda z, y, x, c: (z, y, 1 - x, c))
ALONG_C = moves(lambda z, y, x, c: (z, y, x, 1 - c))


def move(x, pairs):
    return lax.ppermute(x, "blk", pairs)


def sync(values, after):
    values, after = list(values), list(after)
    anywhere = pl.BlockSpec(memory_space=pl.ANY)
    return pl.pallas_call(
        lambda *refs: None,
        out_shape=[jax.ShapeDtypeStruct(x.shape, x.dtype) for x in values],
        in_specs=[anywhere] * (len(values) + len(after)),
        out_specs=[anywhere] * len(values),
        input_output_aliases={i: i for i in range(len(values))},
        compiler_params=params(1),
        cost_estimate=cost(0, 0),
        name="sync",
    )(*values, *after)


def other_core(lines):
    return [move(a, ALONG_C) for a in lines]


def piece_order(me):
    c = me % CORES
    x = me // CORES % CHIPS_X
    y = me // (CORES * CHIPS_X) % CHIPS_Y
    z = me // (CORES * CHIPS_X * CHIPS_Y)
    def chip(yy, xx, cc):
        return [
            device_at((z + CHIPS_Z - back) % CHIPS_Z, yy, xx, cc) for back in range(CHIPS_Z)
        ]

    near, corner = [], []
    for cc in (c, 1 - c):
        near.append(chip(y, x, cc) + chip(y, 1 - x, cc) + chip(1 - y, x, cc))
        corner.append(chip(1 - y, 1 - x, cc))
    return jnp.stack(near[0] + near[1] + corner[0] + corner[1]).astype(jnp.int32)


def summed(me, share):
    core, place, z = me % CORES, me // CORES % (CHIPS_Y * CHIPS_X), me // device_at(1, 0, 0, 0)

    def rows(x, at, dim=0):
        return lax.dynamic_index_in_dim(x, at, dim, keepdims=False)

    share = rows(share, core, 2) + move(rows(share, 1 - core, 2), ALONG_C)
    share = (
        rows(share, place)
        + move(rows(share, place ^ 1), ALONG_X)
        + move(rows(share, place ^ CHIPS_X), ALONG_Y)
        + move(rows(share, place ^ (1 + CHIPS_X)), DIAGONAL)
    )
    total = rows(share, z)
    for step in range(1, CHIPS_Z):
        total += move(rows(share, (z + step) % CHIPS_Z), Z_BY[step])
    return total


def one_group(sigma_anc, panels, diag_inv, scaled_parent_panel, struct_upper, struct_lower):
    me = lax.axis_index("blk")
    pos = piece_order(me)
    v = scaled_parent_panel.reshape(LOWER_NODES_2, W, W)
    vt = jnp.transpose(v, (0, 2, 1))
    diag = diag_inv.reshape(UPPER_NODES_1 + LOWER_NODES_2, W, W)
    own_blocks = 2 * me + jnp.arange(2, dtype=jnp.int32)
    on_first = (me == 0).astype(jnp.int32)[None]

    def owns(row):
        return jnp.any(row[None, :] == own_blocks[:, None], axis=1).astype(jnp.int32)

    def finish_upper(j, gathered):
        zt = product(struct_upper[j], sigma_anc, gathered, 1, j)
        return upper(j, upper_flags[j], pos, zt, pieces, upper_diag[j], v[j], vt[j])

    def both_cores(lines):
        return lines + other_core(lines)

    low_blocks = struct_lower.reshape(SLOTS)
    pieces = transposed_pieces(panels, 0, 4)
    spread = lax.all_to_all(pieces, "blk", 0, 0, tiled=True).reshape(-1, SUB, W)

    def offsets(blocks, which):
        return 8 * (blocks // 2) + 2 * which + blocks % 2

    which = jnp.arange(LOWER_NODES_2, dtype=jnp.int32)[:, None]
    upper_flags = [
        jnp.concatenate([owns(struct_upper[j]), owns(struct_lower[j]), on_first])
        for j in range(UPPER_NODES_1)
    ]
    upper_diag = [jnp.stack([diag[j], diag[UPPER_NODES_1 + j]]) for j in range(UPPER_NODES_1)]
    lower_flags = jnp.concatenate([owns(struct_lower[0]), owns(struct_lower[1])])
    own = picked(offsets(struct_upper, which).reshape(-1), spread)
    own_low = picked(offsets(struct_lower, UPPER_NODES_1 + which).reshape(-1), spread)
    small = upper_flags + upper_diag + [v[0], v[1], vt[0], vt[1], lower_flags, pos, low_blocks]
    (own,) = sync([own], small)
    v, vt = small[4:6], small[6:8]

    lines, xs, ys = [own], [], []
    far_lines, far_xs, far_ys = [], [], []
    for step in range(CHIPS_Z - 1):
        moved = [move(lines[-1], d) for d in (ALONG_Z, ALONG_X, ALONG_Y)]
        swapped = [move(lines[-1], ALONG_C)]
        if step > 0:
            swapped.append(move(xs[-1] if step == 1 else ys[0], ALONG_C))
        if step == 0:
            line, x, y, own_low = sync(moved + [own_low], swapped)
        else:
            line, x, y = sync(moved, swapped)
        lines, xs, ys = lines + [line], xs + [x], ys + [y]
        far_lines.append(swapped[0])
        if step > 0:
            (far_xs if step == 1 else far_ys).append(swapped[1])
    moved = [
        move(lines[3], ALONG_X),
        move(lines[3], ALONG_Y),
        move(ys[0], ALONG_X),
        move(xs[1], ALONG_Y),
        move(own_low, ALONG_Z),
    ]
    swapped = other_core([lines[3], xs[1], ys[1], xs[2], ys[2]])
    x3, y3, d0, d1, behind = sync(moved, swapped)
    far_lines.append(swapped[0])
    far_xs += swapped[1::2]
    far_ys += swapped[2::2]
    xs, ys = xs + [x3], ys + [y3]
    moved = [
        move(ys[2], ALONG_X),
        move(xs[3], ALONG_Y),
        move(behind, ALONG_Z),
        move(own_low, AGAINST_Z),
        jnp.concatenate([own_low, behind]),
    ]
    swapped = other_core([xs[3], ys[3], d0, d1])
    d2, d3, across, before, first_pair = sync(moved, swapped)
    far_xs.append(swapped[0])
    far_ys.append(swapped[1])
    gathered = lines + xs + ys + far_lines + far_xs + far_ys
    gathered += [d0, d1, d2, d3, swapped[2], swapped[3], *other_core([d2, d3])]

    s = [first_pair, jnp.concatenate([across, before])]
    sides = [move(a, ALONG_X) for a in s] + [move(a, ALONG_Y) for a in s]
    up0 = finish_upper(0, gathered)
    sides = list(sync(sides, [up0[2]]))
    corner = [move(sides[2], ALONG_X), move(sides[1], ALONG_Y)]
    near = both_cores(s + sides)
    up1 = finish_upper(1, gathered)
    corner = list(sync(corner, [up1[2], *near]))
    zt = product(low_blocks, sigma_anc, near + both_cores(corner), LOWER_NODES_2, mib=60)
    panel, late = lower(lower_flags, pos, [zt], pieces, (up0, up1))
    by_device = (CHIPS_Z, CHIPS_Y * CHIPS_X, CORES, -1, W)
    diag_share = jnp.concatenate([up0[2], up1[2], late]).reshape(by_device)
    parent_share = jnp.concatenate([up0[3], up1[3]]).reshape(by_device)
    total = summed(me, jnp.swapaxes(jnp.concatenate([diag_share, parent_share], axis=3), 0, 1))
    diag_rows = diag_share.shape[3]
    return panel, total[:diag_rows], total[diag_rows:]


def block_table(struct_upper, struct_lower, blocks):
    ids = jnp.arange(blocks, dtype=jnp.int32)
    upper = jnp.any(struct_upper[:, :, None] == ids[None, None, :], axis=1)
    lower = jnp.any(struct_lower[:, :, None] == ids[None, None, :], axis=1)
    return jnp.concatenate([upper, lower], axis=0).astype(jnp.float32)


def row_mask(table, first_row, count):
    blocks = table.shape[1]
    rows = first_row + jnp.arange(count, dtype=jnp.int32)
    membership_grid = (
        (rows // NODE_WIDTH)[:, None] == jnp.arange(blocks, dtype=jnp.int32)[None, :]
    ).astype(jnp.float32)
    return jnp.dot(
        membership_grid, table.T, precision=HIGH_ACCURACY, preferred_element_type=jnp.float32
    )


def strip_summands(reciprocal_lines, array_lines, membership_grid, stacked_arrays):
    count = reciprocal_lines.shape[0]
    upper_width_1 = UPPER_NODES_1 * NODE_WIDTH
    matrix_columns = jnp.repeat(array_lines, NODE_WIDTH, axis=1)
    g_up = -(matrix_columns[:, :upper_width_1] * reciprocal_lines[:, :upper_width_1])
    collected_elder_share = jnp.einsum(
        "rjw,cj->rcw",
        g_up.reshape(count, UPPER_NODES_1, NODE_WIDTH),
        membership_grid,
        precision=HIGH_ACCURACY,
    )
    resolved_bottom_share = matrix_columns[:, upper_width_1:].reshape(
        count, LOWER_NODES_2, NODE_WIDTH
    ) * (
        jnp.einsum("odf,dfy->ody", collected_elder_share, stacked_arrays, precision=HIGH_ACCURACY)
        + reciprocal_lines[:, upper_width_1:].reshape(count, LOWER_NODES_2, NODE_WIDTH)
    )
    strip_result = jnp.concatenate(
        [g_up, -resolved_bottom_share.reshape(count, LOWER_NODES_2 * NODE_WIDTH)], axis=1
    )
    return (strip_result, collected_elder_share, resolved_bottom_share)


def block_sums(urows, reciprocal_lines, collected_elder_share, resolved_bottom_share):
    count = urows.shape[0]
    upper_width_1 = UPPER_NODES_1 * NODE_WIDTH
    u_up = urows[:, :upper_width_1].reshape(count, UPPER_NODES_1, NODE_WIDTH)
    u_low = urows[:, upper_width_1:].reshape(count, LOWER_NODES_2, NODE_WIDTH)
    amat = jnp.einsum(
        "rjw,rjv->jwv",
        u_up,
        reciprocal_lines[:, :upper_width_1].reshape(count, UPPER_NODES_1, NODE_WIDTH),
        precision=HIGH_ACCURACY,
    )
    block_matrix = jnp.einsum("rcw,rcv->cwv", u_low, collected_elder_share, precision=HIGH_ACCURACY)
    extra_matrix = jnp.einsum("rcw,rcv->cwv", u_low, resolved_bottom_share, precision=HIGH_ACCURACY)
    return jnp.concatenate([amat, block_matrix, extra_matrix], axis=0)


def per_device(sigma_anc, panels, diag_inv, scaled_parent_panel, struct_upper, struct_lower):
    rows_grp, cols_dev = sigma_anc.shape
    rows_dev = panels.shape[0]
    grp_count = lax.axis_size("grp")
    blk_count = lax.axis_size("blk")
    grp_pos = lax.axis_index("grp")
    blk_pos = lax.axis_index("blk")
    blocks = cols_dev * blk_count // NODE_WIDTH
    table = block_table(struct_upper, struct_lower, blocks)
    parent_ids = jnp.arange(LOWER_NODES_2, dtype=jnp.int32) % UPPER_NODES_1
    membership_grid = (
        parent_ids[:, None] == jnp.arange(UPPER_NODES_1, dtype=jnp.int32)[None, :]
    ).astype(jnp.float32)
    stacked_arrays = scaled_parent_panel.reshape(LOWER_NODES_2, NODE_WIDTH, NODE_WIDTH)
    first_in = grp_pos * rows_grp + blk_pos * rows_dev
    upanel = panels * jnp.repeat(row_mask(table, first_in, rows_dev), NODE_WIDTH, axis=1)
    grouped = lax.all_gather(upanel, "blk", axis=0, tiled=True)
    partial_value = lax.dot_general(
        sigma_anc,
        grouped,
        (((0,), (0,)), ((), ())),
        precision=HIGH_ACCURACY,
        preferred_element_type=jnp.float32,
    )
    share = cols_dev // grp_count
    col_first = blk_pos * cols_dev
    root = col_first // rows_grp
    offset = jnp.clip(col_first - grp_pos * rows_grp, 0, rows_grp - cols_dev)
    own_first = col_first + grp_pos * share
    owned_mask = row_mask(table, own_first, share)
    nterms = UPPER_NODES_1 + 2 * LOWER_NODES_2
    inverse_columns = lax.psum(partial_value, "grp")
    inverse_owned = lax.dynamic_slice_in_dim(inverse_columns, grp_pos * share, share, 0)
    strip_result, collected_elder_share, resolved_bottom_share = strip_summands(
        inverse_owned, owned_mask, membership_grid, stacked_arrays
    )

    def on_root():
        u_cols = lax.dynamic_slice_in_dim(grouped, offset, cols_dev, 0)
        complete_mask = row_mask(table, col_first, cols_dev)
        discarded_result, collected_entire_factor, resolved_entire_factor = strip_summands(
            inverse_columns, complete_mask, membership_grid, stacked_arrays
        )
        return block_sums(u_cols, inverse_columns, collected_entire_factor, resolved_entire_factor)

    def off_root():
        return jnp.zeros((nterms, NODE_WIDTH, NODE_WIDTH), jnp.float32)

    terms = lax.cond(grp_pos == root, on_root, off_root)
    summed = lax.psum(terms, ("grp", "blk"))
    amat = summed[:UPPER_NODES_1]
    block_matrix = summed[UPPER_NODES_1 : UPPER_NODES_1 + LOWER_NODES_2]
    extra_matrix = summed[UPPER_NODES_1 + LOWER_NODES_2 :]
    diagonal_matrices = diag_inv.reshape(UPPER_NODES_1 + LOWER_NODES_2, NODE_WIDTH, NODE_WIDTH)
    s_up = diagonal_matrices[:UPPER_NODES_1] + amat
    parent_selection = jnp.einsum("cj,jwv->cwv", membership_grid, s_up, precision=HIGH_ACCURACY)
    solved_parent = jnp.einsum(
        "ghz,gzs->ghs", parent_selection, stacked_arrays, precision=HIGH_ACCURACY
    ) + jnp.transpose(block_matrix, (0, 2, 1))
    lower_selection = (
        diagonal_matrices[UPPER_NODES_1:]
        + jnp.einsum("lmt,lmx->ltx", stacked_arrays, solved_parent, precision=HIGH_ACCURACY)
        + extra_matrix
    )
    whole_diag = jnp.concatenate([s_up, lower_selection], axis=0).reshape(
        (UPPER_NODES_1 + LOWER_NODES_2) * NODE_WIDTH, NODE_WIDTH
    )
    whole_parent = -solved_parent.reshape(LOWER_NODES_2 * NODE_WIDTH, NODE_WIDTH)
    diag_rows = (UPPER_NODES_1 + LOWER_NODES_2) * NODE_WIDTH // blk_count
    parent_rows = LOWER_NODES_2 * NODE_WIDTH // blk_count
    cov_diag = lax.dynamic_slice_in_dim(whole_diag, blk_pos * diag_rows, diag_rows, 0)
    cov_parent = lax.dynamic_slice_in_dim(whole_parent, blk_pos * parent_rows, parent_rows, 0)
    return (strip_result, cov_diag, cov_parent)


def solution(mesh):
    single = mesh.shape["grp"] == 1 and mesh.shape["blk"] == PIECES
    return jax.shard_map(
        one_group if single else per_device,
        mesh=mesh,
        in_specs=(P("grp", "blk"), P(("grp", "blk"), None), P(), P(), P(), P()),
        out_specs=(P(("blk", "grp"), None), P("blk", None), P("blk", None)),
        check_vma=False,
    )
```

```python
import jax
import jax.numpy as jnp
from jax import lax
from jax.experimental import pallas as pl
from jax.experimental.pallas import tpu as pltpu
from jax.sharding import PartitionSpec as P

NODE_WIDTH = 256
UPPER_NODES_1 = 2
LOWER_NODES_2 = 2
F32 = jnp.float32
BF16 = jnp.bfloat16


HIGH_ACCURACY = lax.Precision.HIGHEST


CHIPS_Z, CHIPS_Y, CHIPS_X, CORES = 4, 2, 2, 2
PIECES = CHIPS_Z * CHIPS_Y * CHIPS_X * CORES
SUB = NODE_WIDTH // PIECES
SLOTS = 32
PER_STEP = 4
W = NODE_WIDTH


def params(mib):
    return pltpu.CompilerParams(vmem_limit_bytes=mib * 1024 * 1024)


def split(x):
    hi = x.astype(BF16)
    return hi, (x - hi.astype(F32)).astype(BF16)


def dot3(a, b):
    a_hi, a_lo = split(a)
    b_hi, b_lo = split(b)
    small = jnp.dot(a_lo, b_hi, preferred_element_type=F32) + jnp.dot(
        a_hi, b_lo, preferred_element_type=F32
    )
    return jnp.dot(a_hi, b_hi, preferred_element_type=F32) + small


def cost(flops, nbytes):
    return pl.CostEstimate(flops=flops, bytes_accessed=nbytes, transcendentals=0)


def transpose_body(x_ref, o_ref):
    for c in range(o_ref.shape[1]):
        for rb in range(2):
            t = x_ref[rb * W : (rb + 1) * W, c * W : (c + 1) * W].T
            o_ref[:, c, rb] = t.reshape(PIECES, SUB, W)


def transposed_pieces(panels, first, count):
    shape = (PIECES, count, 2, SUB, W)
    return pl.pallas_call(
        transpose_body,
        out_shape=jax.ShapeDtypeStruct(shape, F32),
        grid=(1,),
        in_specs=[pl.BlockSpec((2 * W, count * W), lambda i: (0, first // count))],
        out_specs=pl.BlockSpec(shape, lambda i: (0, 0, 0, 0, 0)),
        compiler_params=params(16),
        cost_estimate=cost(0, 4 * panels.size * count // 2),
        name="transposed_pieces",
    )(panels)


def pick_body(idx_ref, a_ref, o_ref):
    for k in range(o_ref.shape[1]):
        o_ref[0, k] = a_ref[idx_ref[k]]


def picked(idx, a):
    return pl.pallas_call(
        pick_body,
        out_shape=jax.ShapeDtypeStruct((1, idx.shape[0], SUB, W), F32),
        in_specs=[
            pl.BlockSpec(memory_space=pltpu.SMEM),
            pl.BlockSpec(memory_space=pltpu.VMEM),
        ],
        out_specs=pl.BlockSpec(memory_space=pltpu.VMEM),
        compiler_params=params(16),
        cost_estimate=cost(0, 4 * (a.size + idx.size * SUB * W)),
        name="picked",
    )(idx, a)


def product_body(accs, idx_ref, *refs):
    sig, lines, o_ref = refs[:PER_STEP], refs[PER_STEP:-1], refs[-1]
    step = pl.program_id(0)
    per_acc = pl.num_programs(0) // accs
    left = []
    for q in range(PER_STEP):
        left.append(jnp.concatenate([r[:, q].reshape(-1, W) for r in lines], axis=0))
    value = dot3(jnp.concatenate(left, axis=1), jnp.concatenate([r[...] for r in sig], axis=0))

    @pl.when(lax.rem(step, per_acc) == 0)
    def _():
        o_ref[0] = value

    @pl.when(lax.rem(step, per_acc) != 0)
    def _():
        o_ref[0] += value


def product(idx, sigma, pieces, accs, chunk=0, mib=18):
    steps = SLOTS // PER_STEP
    cols = sigma.shape[1]
    rows = SUB * sum(p.shape[0] for p in pieces)

    def sig_spec(q):
        return pl.BlockSpec((W, cols), lambda i, idx, q=q: (idx[i * PER_STEP + q], 0))

    piece_specs = [
        pl.BlockSpec((p.shape[0], PER_STEP, SUB, W), lambda i, idx: (0, i + chunk * steps, 0, 0))
        for p in pieces
    ]
    return pl.pallas_call(
        lambda *refs: product_body(accs, *refs),
        out_shape=jax.ShapeDtypeStruct((accs, rows, cols), F32),
        grid_spec=pltpu.PrefetchScalarGridSpec(
            num_scalar_prefetch=1,
            grid=(steps,),
            in_specs=[sig_spec(q) for q in range(PER_STEP)] + piece_specs,
            out_specs=pl.BlockSpec((1, rows, cols), lambda i, idx: (lax.div(i * accs, steps), 0, 0)),
        ),
        compiler_params=params(mib),
        cost_estimate=cost(6 * SLOTS * rows * W * cols, 4 * SLOTS * W * (cols + rows)),
        name="product",
    )(idx, *([sigma] * PER_STEP), *pieces)


def row_flags(rows, lo, hi):
    top = lax.broadcasted_iota(jnp.int32, (rows, 1), 0) < W
    return jnp.where(top, lo.astype(F32), hi.astype(F32))


def local_lines(ref, c):
    return jnp.concatenate([ref[:, c, rb].reshape(W, W) for rb in range(2)], axis=1)


def in_order(pos_ref, zt_refs, c, scratch):
    g = 0
    for ref in zt_refs:
        for row in range(0, ref.shape[1], SUB):
            at = pl.multiple_of(pos_ref[g] * SUB, SUB)
            scratch[pl.ds(at, SUB), :] = ref[c, row : row + SUB, :]
            g += 1
    return scratch[...].T


def upper_body(flag_ref, pos_ref, zt_ref, up_ref, low_ref, diag_ref, v_ref, vt_ref, *outs):
    g_ref, gv_ref, a_ref, yp_ref, l_ref, scratch = outs
    z = in_order(pos_ref, [zt_ref], 0, scratch)
    g = -z * row_flags(z.shape[0], flag_ref[0], flag_ref[1])
    g_ref[...] = g
    on_first = flag_ref[4].astype(F32)
    a = diag_ref[0] * on_first - dot3(local_lines(up_ref, 0), g)
    a_ref[...] = a
    below = g * row_flags(z.shape[0], flag_ref[2], flag_ref[3])
    gv = dot3(below, v_ref[...])
    gv_ref[...] = gv
    u = local_lines(low_ref, 0)
    yp = dot3(a, v_ref[...]) + dot3(u, below).T
    yp_ref[...] = -yp
    l_ref[...] = dot3(vt_ref[...], yp) + dot3(u, gv) + diag_ref[1] * on_first


def upper(j, flags, pos, zt, pieces, diag, v, vt):
    cols = zt.shape[2]
    square = jax.ShapeDtypeStruct((W, W), F32)
    tall = jax.ShapeDtypeStruct((cols, W), F32)
    def whole(x):
        return pl.BlockSpec(x.shape, lambda i: (0,) * x.ndim)

    def own(s):
        return pl.BlockSpec((PIECES, 1, 2, SUB, W), lambda i: (0, s, 0, 0, 0))

    out_shape = (tall, tall, square, square, square)
    return pl.pallas_call(
        upper_body,
        out_shape=out_shape,
        grid=(1,),
        in_specs=[pl.BlockSpec(memory_space=pltpu.SMEM)] * 2
        + [whole(zt), own(j), own(UPPER_NODES_1 + j), whole(diag), whole(v), whole(vt)],
        out_specs=tuple(whole(o) for o in out_shape),
        scratch_shapes=[pltpu.VMEM((W, cols), F32)],
        compiler_params=params(24),
        cost_estimate=cost(24 * W * W * (cols + W), 4 * W * (6 * cols + 8 * W)),
        name="upper",
    )(flags, pos, zt, pieces, pieces, diag, v, vt)


def lower_body(parts, flag_ref, pos_ref, *refs):
    zt_refs = refs[:parts]
    low_ref, g0, g1, gv0, gv1, l0, l1, panel_ref, late_ref, scratch = refs[parts:]
    for j, g_ref in enumerate((g0, g1)):
        panel_ref[:, j * W : (j + 1) * W] = g_ref[...]
    for c, (gv_ref, l_ref) in enumerate(((gv0, l0), (gv1, l1))):
        z = in_order(pos_ref, zt_refs, c, scratch)
        z = z * row_flags(z.shape[0], flag_ref[2 * c], flag_ref[2 * c + 1])
        col = (UPPER_NODES_1 + c) * W
        panel_ref[:, col : col + W] = -(gv_ref[...] + z)
        late_ref[c * W : (c + 1) * W, :] = l_ref[...] + dot3(local_lines(low_ref, c), z)


def lower(flags, pos, zts, low, ups):
    cols = zts[0].shape[2]
    operands = [ups[j][i] for i in (0, 1, 4) for j in range(UPPER_NODES_1)]
    def whole(x):
        return pl.BlockSpec(x.shape, lambda i: (0,) * x.ndim)

    out_shape = (
        jax.ShapeDtypeStruct((cols, 4 * W), F32),
        jax.ShapeDtypeStruct((LOWER_NODES_2 * W, W), F32),
    )
    return pl.pallas_call(
        lambda *refs: lower_body(len(zts), *refs),
        out_shape=out_shape,
        grid=(1,),
        in_specs=[pl.BlockSpec(memory_space=pltpu.SMEM)] * 2
        + [whole(z) for z in zts]
        + [pl.BlockSpec((PIECES, LOWER_NODES_2, 2, SUB, W), lambda i: (0, 1, 0, 0, 0))]
        + [whole(o) for o in operands],
        out_specs=tuple(whole(o) for o in out_shape),
        scratch_shapes=[pltpu.VMEM((W, cols), F32)],
        compiler_params=params(32),
        cost_estimate=cost(12 * W * W * cols, 4 * W * (12 * cols + 6 * W)),
        name="lower",
    )(flags, pos, *zts, low, *operands)


def device_at(z, y, x, c):
    return ((z * CHIPS_Y + y) * CHIPS_X + x) * CORES + c


def moves(f):
    pairs = []
    for z in range(CHIPS_Z):
        for y in range(CHIPS_Y):
            for x in range(CHIPS_X):
                for c in range(CORES):
                    pairs.append((device_at(z, y, x, c), device_at(*f(z, y, x, c))))
    return pairs


ALONG_Z = moves(lambda z, y, x, c: ((z + 1) % CHIPS_Z, y, x, c))
AGAINST_Z = moves(lambda z, y, x, c: ((z - 1) % CHIPS_Z, y, x, c))
DIAGONAL = moves(lambda z, y, x, c: (z, 1 - y, 1 - x, c))
Z_BY = [moves(lambda z, y, x, c, s=s: ((z + s) % CHIPS_Z, y, x, c)) for s in range(CHIPS_Z)]
ALONG_Y = moves(lambda z, y, x, c: (z, 1 - y, x, c))
ALONG_X = moves(lambda z, y, x, c: (z, y, 1 - x, c))
ALONG_C = moves(lambda z, y, x, c: (z, y, x, 1 - c))


def move(x, pairs):
    return lax.ppermute(x, "blk", pairs)


def sync(values, after):
    values, after = list(values), list(after)
    anywhere = pl.BlockSpec(memory_space=pl.ANY)
    return pl.pallas_call(
        lambda *refs: None,
        out_shape=[jax.ShapeDtypeStruct(x.shape, x.dtype) for x in values],
        in_specs=[anywhere] * (len(values) + len(after)),
        out_specs=[anywhere] * len(values),
        input_output_aliases={i: i for i in range(len(values))},
        compiler_params=params(1),
        cost_estimate=cost(0, 0),
        name="sync",
    )(*values, *after)


def other_core(lines):
    return [move(a, ALONG_C) for a in lines]


def piece_order(me):
    c = me % CORES
    x = me // CORES % CHIPS_X
    y = me // (CORES * CHIPS_X) % CHIPS_Y
    z = me // (CORES * CHIPS_X * CHIPS_Y)
    def chip(yy, xx, cc):
        return [
            device_at((z + CHIPS_Z - back) % CHIPS_Z, yy, xx, cc) for back in range(CHIPS_Z)
        ]

    near, corner = [], []
    for cc in (c, 1 - c):
        near.append(chip(y, x, cc) + chip(y, 1 - x, cc) + chip(1 - y, x, cc))
        corner.append(chip(1 - y, 1 - x, cc))
    return jnp.stack(near[0] + near[1] + corner[0] + corner[1]).astype(jnp.int32)


def summed(me, share):
    core, place, z = me % CORES, me // CORES % (CHIPS_Y * CHIPS_X), me // device_at(1, 0, 0, 0)

    def rows(x, at, dim=0):
        return lax.dynamic_index_in_dim(x, at, dim, keepdims=False)

    share = rows(share, core, 2) + move(rows(share, 1 - core, 2), ALONG_C)
    share = (
        rows(share, place)
        + move(rows(share, place ^ 1), ALONG_X)
        + move(rows(share, place ^ CHIPS_X), ALONG_Y)
        + move(rows(share, place ^ (1 + CHIPS_X)), DIAGONAL)
    )
    total = rows(share, z)
    for step in range(1, CHIPS_Z):
        total += move(rows(share, (z + step) % CHIPS_Z), Z_BY[step])
    return total


def one_group(sigma_anc, panels, diag_inv, scaled_parent_panel, struct_upper, struct_lower):
    me = lax.axis_index("blk")
    pos = piece_order(me)
    v = scaled_parent_panel.reshape(LOWER_NODES_2, W, W)
    vt = jnp.transpose(v, (0, 2, 1))
    diag = diag_inv.reshape(UPPER_NODES_1 + LOWER_NODES_2, W, W)
    own_blocks = 2 * me + jnp.arange(2, dtype=jnp.int32)
    on_first = (me == 0).astype(jnp.int32)[None]

    def owns(row):
        return jnp.any(row[None, :] == own_blocks[:, None], axis=1).astype(jnp.int32)

    def finish_upper(j, zt):
        return upper(j, upper_flags[j], pos, zt, pieces, upper_diag[j], v[j], vt[j])

    def both_cores(lines):
        return lines + other_core(lines)

    low_blocks = struct_lower.reshape(SLOTS)
    pieces = transposed_pieces(panels, 0, 4)
    spread = lax.all_to_all(pieces, "blk", 0, 0, tiled=True).reshape(-1, SUB, W)

    def offsets(blocks, which):
        return 8 * (blocks // 2) + 2 * which + blocks % 2

    which = jnp.arange(LOWER_NODES_2, dtype=jnp.int32)[:, None]
    upper_flags = [
        jnp.concatenate([owns(struct_upper[j]), owns(struct_lower[j]), on_first])
        for j in range(UPPER_NODES_1)
    ]
    upper_diag = [jnp.stack([diag[j], diag[UPPER_NODES_1 + j]]) for j in range(UPPER_NODES_1)]
    lower_flags = jnp.concatenate([owns(struct_lower[0]), owns(struct_lower[1])])
    own = picked(offsets(struct_upper, which).reshape(-1), spread)
    own_low = picked(offsets(struct_lower, UPPER_NODES_1 + which).reshape(-1), spread)
    small = upper_flags + upper_diag + [v[0], v[1], vt[0], vt[1], lower_flags, pos, low_blocks]
    (own,) = sync([own], small)
    v, vt = small[4:6], small[6:8]

    lines, xs, ys = [own], [], []
    far_lines, far_xs, far_ys = [], [], []
    for step in range(CHIPS_Z - 1):
        moved = [move(lines[-1], d) for d in (ALONG_Z, ALONG_X, ALONG_Y)]
        swapped = [move(lines[-1], ALONG_C)]
        if step > 0:
            swapped.append(move(xs[-1] if step == 1 else ys[0], ALONG_C))
        if step == 0:
            line, x, y, own_low = sync(moved + [own_low], swapped)
        else:
            line, x, y = sync(moved, swapped)
        lines, xs, ys = lines + [line], xs + [x], ys + [y]
        far_lines.append(swapped[0])
        if step > 0:
            (far_xs if step == 1 else far_ys).append(swapped[1])
    moved = [
        move(lines[3], ALONG_X),
        move(lines[3], ALONG_Y),
        move(ys[0], ALONG_X),
        move(xs[1], ALONG_Y),
        move(own_low, ALONG_Z),
    ]
    swapped = other_core([lines[3], xs[1], ys[1], xs[2], ys[2]])
    x3, y3, d0, d1, behind = sync(moved, swapped)
    far_lines.append(swapped[0])
    far_xs += swapped[1::2]
    far_ys += swapped[2::2]
    xs, ys = xs + [x3], ys + [y3]
    moved = [
        move(ys[2], ALONG_X),
        move(xs[3], ALONG_Y),
        move(behind, ALONG_Z),
        move(own_low, AGAINST_Z),
        jnp.concatenate([own_low, behind]),
    ]
    swapped = other_core([xs[3], ys[3], d0, d1])
    d2, d3, across, before, first_pair = sync(moved, swapped)
    far_xs.append(swapped[0])
    far_ys.append(swapped[1])
    gathered = lines + xs + ys + far_lines + far_xs + far_ys
    gathered += [d0, d1, d2, d3, swapped[2], swapped[3], *other_core([d2, d3])]

    s = [first_pair, jnp.concatenate([across, before])]
    tx = [move(a, ALONG_X) for a in s]
    ty = [move(a, ALONG_Y) for a in s]
    zt0 = product(struct_upper[0], sigma_anc, gathered, 1, 0)
    zt1 = product(struct_upper[1], sigma_anc, gathered, 1, 1)
    far_s = other_core(s)
    *sides, zt0, zt1 = sync([*tx, *ty, zt0, zt1], far_s)
    tx, ty = sides[:2], sides[2:]
    corner = [move(ty[0], ALONG_X), move(tx[1], ALONG_Y)]
    up0, up1 = finish_upper(0, zt0), finish_upper(1, zt1)
    near = s + sides + far_s + other_core(sides)
    corner = list(sync(corner, [up0[2], up1[2], *near]))
    zt = product(low_blocks, sigma_anc, near + both_cores(corner), LOWER_NODES_2, mib=60)
    panel, late = lower(lower_flags, pos, [zt], pieces, (up0, up1))
    by_device = (CHIPS_Z, CHIPS_Y * CHIPS_X, CORES, -1, W)
    diag_share = jnp.concatenate([up0[2], up1[2], late]).reshape(by_device)
    parent_share = jnp.concatenate([up0[3], up1[3]]).reshape(by_device)
    total = summed(me, jnp.swapaxes(jnp.concatenate([diag_share, parent_share], axis=3), 0, 1))
    diag_rows = diag_share.shape[3]
    return panel, total[:diag_rows], total[diag_rows:]


def block_table(struct_upper, struct_lower, blocks):
    ids = jnp.arange(blocks, dtype=jnp.int32)
    upper = jnp.any(struct_upper[:, :, None] == ids[None, None, :], axis=1)
    lower = jnp.any(struct_lower[:, :, None] == ids[None, None, :], axis=1)
    return jnp.concatenate([upper, lower], axis=0).astype(jnp.float32)


def row_mask(table, first_row, count):
    blocks = table.shape[1]
    rows = first_row + jnp.arange(count, dtype=jnp.int32)
    membership_grid = (
        (rows // NODE_WIDTH)[:, None] == jnp.arange(blocks, dtype=jnp.int32)[None, :]
    ).astype(jnp.float32)
    return jnp.dot(
        membership_grid, table.T, precision=HIGH_ACCURACY, preferred_element_type=jnp.float32
    )


def strip_summands(reciprocal_lines, array_lines, membership_grid, stacked_arrays):
    count = reciprocal_lines.shape[0]
    upper_width_1 = UPPER_NODES_1 * NODE_WIDTH
    matrix_columns = jnp.repeat(array_lines, NODE_WIDTH, axis=1)
    g_up = -(matrix_columns[:, :upper_width_1] * reciprocal_lines[:, :upper_width_1])
    collected_elder_share = jnp.einsum(
        "rjw,cj->rcw",
        g_up.reshape(count, UPPER_NODES_1, NODE_WIDTH),
        membership_grid,
        precision=HIGH_ACCURACY,
    )
    resolved_bottom_share = matrix_columns[:, upper_width_1:].reshape(
        count, LOWER_NODES_2, NODE_WIDTH
    ) * (
        jnp.einsum("odf,dfy->ody", collected_elder_share, stacked_arrays, precision=HIGH_ACCURACY)
        + reciprocal_lines[:, upper_width_1:].reshape(count, LOWER_NODES_2, NODE_WIDTH)
    )
    strip_result = jnp.concatenate(
        [g_up, -resolved_bottom_share.reshape(count, LOWER_NODES_2 * NODE_WIDTH)], axis=1
    )
    return (strip_result, collected_elder_share, resolved_bottom_share)


def block_sums(urows, reciprocal_lines, collected_elder_share, resolved_bottom_share):
    count = urows.shape[0]
    upper_width_1 = UPPER_NODES_1 * NODE_WIDTH
    u_up = urows[:, :upper_width_1].reshape(count, UPPER_NODES_1, NODE_WIDTH)
    u_low = urows[:, upper_width_1:].reshape(count, LOWER_NODES_2, NODE_WIDTH)
    amat = jnp.einsum(
        "rjw,rjv->jwv",
        u_up,
        reciprocal_lines[:, :upper_width_1].reshape(count, UPPER_NODES_1, NODE_WIDTH),
        precision=HIGH_ACCURACY,
    )
    block_matrix = jnp.einsum("rcw,rcv->cwv", u_low, collected_elder_share, precision=HIGH_ACCURACY)
    extra_matrix = jnp.einsum("rcw,rcv->cwv", u_low, resolved_bottom_share, precision=HIGH_ACCURACY)
    return jnp.concatenate([amat, block_matrix, extra_matrix], axis=0)


def per_device(sigma_anc, panels, diag_inv, scaled_parent_panel, struct_upper, struct_lower):
    rows_grp, cols_dev = sigma_anc.shape
    rows_dev = panels.shape[0]
    grp_count = lax.axis_size("grp")
    blk_count = lax.axis_size("blk")
    grp_pos = lax.axis_index("grp")
    blk_pos = lax.axis_index("blk")
    blocks = cols_dev * blk_count // NODE_WIDTH
    table = block_table(struct_upper, struct_lower, blocks)
    parent_ids = jnp.arange(LOWER_NODES_2, dtype=jnp.int32) % UPPER_NODES_1
    membership_grid = (
        parent_ids[:, None] == jnp.arange(UPPER_NODES_1, dtype=jnp.int32)[None, :]
    ).astype(jnp.float32)
    stacked_arrays = scaled_parent_panel.reshape(LOWER_NODES_2, NODE_WIDTH, NODE_WIDTH)
    first_in = grp_pos * rows_grp + blk_pos * rows_dev
    upanel = panels * jnp.repeat(row_mask(table, first_in, rows_dev), NODE_WIDTH, axis=1)
    grouped = lax.all_gather(upanel, "blk", axis=0, tiled=True)
    partial_value = lax.dot_general(
        sigma_anc,
        grouped,
        (((0,), (0,)), ((), ())),
        precision=HIGH_ACCURACY,
        preferred_element_type=jnp.float32,
    )
    share = cols_dev // grp_count
    col_first = blk_pos * cols_dev
    root = col_first // rows_grp
    offset = jnp.clip(col_first - grp_pos * rows_grp, 0, rows_grp - cols_dev)
    own_first = col_first + grp_pos * share
    owned_mask = row_mask(table, own_first, share)
    nterms = UPPER_NODES_1 + 2 * LOWER_NODES_2
    inverse_columns = lax.psum(partial_value, "grp")
    inverse_owned = lax.dynamic_slice_in_dim(inverse_columns, grp_pos * share, share, 0)
    strip_result, collected_elder_share, resolved_bottom_share = strip_summands(
        inverse_owned, owned_mask, membership_grid, stacked_arrays
    )

    def on_root():
        u_cols = lax.dynamic_slice_in_dim(grouped, offset, cols_dev, 0)
        complete_mask = row_mask(table, col_first, cols_dev)
        discarded_result, collected_entire_factor, resolved_entire_factor = strip_summands(
            inverse_columns, complete_mask, membership_grid, stacked_arrays
        )
        return block_sums(u_cols, inverse_columns, collected_entire_factor, resolved_entire_factor)

    def off_root():
        return jnp.zeros((nterms, NODE_WIDTH, NODE_WIDTH), jnp.float32)

    terms = lax.cond(grp_pos == root, on_root, off_root)
    summed = lax.psum(terms, ("grp", "blk"))
    amat = summed[:UPPER_NODES_1]
    block_matrix = summed[UPPER_NODES_1 : UPPER_NODES_1 + LOWER_NODES_2]
    extra_matrix = summed[UPPER_NODES_1 + LOWER_NODES_2 :]
    diagonal_matrices = diag_inv.reshape(UPPER_NODES_1 + LOWER_NODES_2, NODE_WIDTH, NODE_WIDTH)
    s_up = diagonal_matrices[:UPPER_NODES_1] + amat
    parent_selection = jnp.einsum("cj,jwv->cwv", membership_grid, s_up, precision=HIGH_ACCURACY)
    solved_parent = jnp.einsum(
        "ghz,gzs->ghs", parent_selection, stacked_arrays, precision=HIGH_ACCURACY
    ) + jnp.transpose(block_matrix, (0, 2, 1))
    lower_selection = (
        diagonal_matrices[UPPER_NODES_1:]
        + jnp.einsum("lmt,lmx->ltx", stacked_arrays, solved_parent, precision=HIGH_ACCURACY)
        + extra_matrix
    )
    whole_diag = jnp.concatenate([s_up, lower_selection], axis=0).reshape(
        (UPPER_NODES_1 + LOWER_NODES_2) * NODE_WIDTH, NODE_WIDTH
    )
    whole_parent = -solved_parent.reshape(LOWER_NODES_2 * NODE_WIDTH, NODE_WIDTH)
    diag_rows = (UPPER_NODES_1 + LOWER_NODES_2) * NODE_WIDTH // blk_count
    parent_rows = LOWER_NODES_2 * NODE_WIDTH // blk_count
    cov_diag = lax.dynamic_slice_in_dim(whole_diag, blk_pos * diag_rows, diag_rows, 0)
    cov_parent = lax.dynamic_slice_in_dim(whole_parent, blk_pos * parent_rows, parent_rows, 0)
    return (strip_result, cov_diag, cov_parent)


def solution(mesh):
    single = mesh.shape["grp"] == 1 and mesh.shape["blk"] == PIECES
    return jax.shard_map(
        one_group if single else per_device,
        mesh=mesh,
        in_specs=(P("grp", "blk"), P(("grp", "blk"), None), P(), P(), P(), P()),
        out_specs=(P(("blk", "grp"), None), P("blk", None), P("blk", None)),
        check_vma=False,
    )
```

```python
import jax
import jax.numpy as jnp
from jax import lax
from jax.experimental import pallas as pl
from jax.experimental.pallas import tpu as pltpu
from jax.sharding import PartitionSpec as P

NODE_WIDTH = 256
UPPER_NODES_1 = 2
LOWER_NODES_2 = 2
F32 = jnp.float32
BF16 = jnp.bfloat16


HIGH_ACCURACY = lax.Precision.HIGHEST


CHIPS_Z, CHIPS_Y, CHIPS_X, CORES = 4, 2, 2, 2
PIECES = CHIPS_Z * CHIPS_Y * CHIPS_X * CORES
SUB = NODE_WIDTH // PIECES
SLOTS = 32
PER_STEP = 4
W = NODE_WIDTH


def params(mib):
    return pltpu.CompilerParams(vmem_limit_bytes=mib * 1024 * 1024)


def split(x):
    hi = x.astype(BF16)
    return hi, (x - hi.astype(F32)).astype(BF16)


def dot3(a, b):
    a_hi, a_lo = split(a)
    b_hi, b_lo = split(b)
    small = jnp.dot(a_lo, b_hi, preferred_element_type=F32) + jnp.dot(
        a_hi, b_lo, preferred_element_type=F32
    )
    return jnp.dot(a_hi, b_hi, preferred_element_type=F32) + small


def cost(flops, nbytes):
    return pl.CostEstimate(flops=flops, bytes_accessed=nbytes, transcendentals=0)


def transpose_body(x_ref, o_ref):
    for c in range(o_ref.shape[1]):
        for rb in range(2):
            t = x_ref[rb * W : (rb + 1) * W, c * W : (c + 1) * W].T
            o_ref[:, c, rb] = t.reshape(PIECES, SUB, W)


def transposed_pieces(panels, first, count):
    shape = (PIECES, count, 2, SUB, W)
    return pl.pallas_call(
        transpose_body,
        out_shape=jax.ShapeDtypeStruct(shape, F32),
        grid=(1,),
        in_specs=[pl.BlockSpec((2 * W, count * W), lambda i: (0, first // count))],
        out_specs=pl.BlockSpec(shape, lambda i: (0, 0, 0, 0, 0)),
        compiler_params=params(16),
        cost_estimate=cost(0, 4 * panels.size * count // 2),
        name="transposed_pieces",
    )(panels)


def pick_body(idx_ref, a_ref, o_ref):
    for k in range(o_ref.shape[1]):
        o_ref[0, k] = a_ref[idx_ref[k]]


def picked(idx, a):
    return pl.pallas_call(
        pick_body,
        out_shape=jax.ShapeDtypeStruct((1, idx.shape[0], SUB, W), F32),
        in_specs=[
            pl.BlockSpec(memory_space=pltpu.SMEM),
            pl.BlockSpec(memory_space=pltpu.VMEM),
        ],
        out_specs=pl.BlockSpec(memory_space=pltpu.VMEM),
        compiler_params=params(16),
        cost_estimate=cost(0, 4 * (a.size + idx.size * SUB * W)),
        name="picked",
    )(idx, a)


def product_body(accs, idx_ref, *refs):
    sig, lines, o_ref = refs[:PER_STEP], refs[PER_STEP:-1], refs[-1]
    step = pl.program_id(0)
    per_acc = pl.num_programs(0) // accs
    left = []
    for q in range(PER_STEP):
        left.append(jnp.concatenate([r[:, q].reshape(-1, W) for r in lines], axis=0))
    value = dot3(jnp.concatenate(left, axis=1), jnp.concatenate([r[...] for r in sig], axis=0))

    @pl.when(lax.rem(step, per_acc) == 0)
    def _():
        o_ref[0] = value

    @pl.when(lax.rem(step, per_acc) != 0)
    def _():
        o_ref[0] += value


def product(idx, sigma, pieces, accs, chunk=0, mib=18):
    steps = SLOTS // PER_STEP
    cols = sigma.shape[1]
    rows = SUB * sum(p.shape[0] for p in pieces)

    def sig_spec(q):
        return pl.BlockSpec((W, cols), lambda i, idx, q=q: (idx[i * PER_STEP + q], 0))

    piece_specs = [
        pl.BlockSpec((p.shape[0], PER_STEP, SUB, W), lambda i, idx: (0, i + chunk * steps, 0, 0))
        for p in pieces
    ]
    return pl.pallas_call(
        lambda *refs: product_body(accs, *refs),
        out_shape=jax.ShapeDtypeStruct((accs, rows, cols), F32),
        grid_spec=pltpu.PrefetchScalarGridSpec(
            num_scalar_prefetch=1,
            grid=(steps,),
            in_specs=[sig_spec(q) for q in range(PER_STEP)] + piece_specs,
            out_specs=pl.BlockSpec((1, rows, cols), lambda i, idx: (lax.div(i * accs, steps), 0, 0)),
        ),
        compiler_params=params(mib),
        cost_estimate=cost(6 * SLOTS * rows * W * cols, 4 * SLOTS * W * (cols + rows)),
        name="product",
    )(idx, *([sigma] * PER_STEP), *pieces)


def row_flags(rows, lo, hi):
    top = lax.broadcasted_iota(jnp.int32, (rows, 1), 0) < W
    return jnp.where(top, lo.astype(F32), hi.astype(F32))


def local_lines(ref, c):
    return jnp.concatenate([ref[:, c, rb].reshape(W, W) for rb in range(2)], axis=1)


def in_order(pos_ref, zt_refs, c, scratch):
    g = 0
    for ref in zt_refs:
        for row in range(0, ref.shape[1], SUB):
            at = pl.multiple_of(pos_ref[g] * SUB, SUB)
            scratch[pl.ds(at, SUB), :] = ref[c, row : row + SUB, :]
            g += 1
    return scratch[...].T


def upper_body(flag_ref, pos_ref, zt_ref, up_ref, low_ref, diag_ref, low_diag_ref, v_ref, *outs):
    g_ref, gv_ref, a_ref, yp_ref, l_ref, scratch = outs
    z = in_order(pos_ref, [zt_ref], 0, scratch)
    g = -z * row_flags(z.shape[0], flag_ref[0], flag_ref[1])
    g_ref[...] = g
    on_first = flag_ref[4].astype(F32)
    a = diag_ref[...] * on_first - dot3(local_lines(up_ref, 0), g)
    a_ref[...] = a
    below = g * row_flags(z.shape[0], flag_ref[2], flag_ref[3])
    gv = dot3(below, v_ref[...])
    gv_ref[...] = gv
    u = local_lines(low_ref, 0)
    yp = dot3(a, v_ref[...]) + dot3(u, below).T
    yp_ref[...] = -yp
    l_ref[...] = dot3(v_ref[...].T, yp) + dot3(u, gv) + low_diag_ref[...] * on_first


def upper(j, flags, pos, zt, pieces, diag, v):
    cols = zt.shape[2]
    square = jax.ShapeDtypeStruct((W, W), F32)
    tall = jax.ShapeDtypeStruct((cols, W), F32)
    def whole(x):
        return pl.BlockSpec(x.shape, lambda i: (0,) * x.ndim)

    def own(s):
        return pl.BlockSpec((PIECES, 1, 2, SUB, W), lambda i: (0, s, 0, 0, 0))

    def block(s):
        return pl.BlockSpec((W, W), lambda i: (s, 0))

    out_shape = (tall, tall, square, square, square)
    return pl.pallas_call(
        upper_body,
        out_shape=out_shape,
        grid=(1,),
        in_specs=[pl.BlockSpec(memory_space=pltpu.SMEM)] * 2
        + [whole(zt), own(j), own(UPPER_NODES_1 + j), block(j), block(UPPER_NODES_1 + j), block(j)],
        out_specs=tuple(whole(o) for o in out_shape),
        scratch_shapes=[pltpu.VMEM((W, cols), F32)],
        compiler_params=params(24),
        cost_estimate=cost(24 * W * W * (cols + W), 4 * W * (6 * cols + 8 * W)),
        name="upper",
    )(flags, pos, zt, pieces, pieces, diag, diag, v)


def lower_body(parts, flag_ref, pos_ref, *refs):
    zt_refs = refs[:parts]
    low_ref, g0, g1, gv0, gv1, l0, l1, panel_ref, late_ref, scratch = refs[parts:]
    for j, g_ref in enumerate((g0, g1)):
        panel_ref[:, j * W : (j + 1) * W] = g_ref[...]
    for c, (gv_ref, l_ref) in enumerate(((gv0, l0), (gv1, l1))):
        z = in_order(pos_ref, zt_refs, c, scratch)
        z = z * row_flags(z.shape[0], flag_ref[2 * c], flag_ref[2 * c + 1])
        col = (UPPER_NODES_1 + c) * W
        panel_ref[:, col : col + W] = -(gv_ref[...] + z)
        late_ref[c * W : (c + 1) * W, :] = l_ref[...] + dot3(local_lines(low_ref, c), z)


def lower(flags, pos, zts, low, ups):
    cols = zts[0].shape[2]
    operands = [ups[j][i] for i in (0, 1, 4) for j in range(UPPER_NODES_1)]
    def whole(x):
        return pl.BlockSpec(x.shape, lambda i: (0,) * x.ndim)

    out_shape = (
        jax.ShapeDtypeStruct((cols, 4 * W), F32),
        jax.ShapeDtypeStruct((LOWER_NODES_2 * W, W), F32),
    )
    return pl.pallas_call(
        lambda *refs: lower_body(len(zts), *refs),
        out_shape=out_shape,
        grid=(1,),
        in_specs=[pl.BlockSpec(memory_space=pltpu.SMEM)] * 2
        + [whole(z) for z in zts]
        + [pl.BlockSpec((PIECES, LOWER_NODES_2, 2, SUB, W), lambda i: (0, 1, 0, 0, 0))]
        + [whole(o) for o in operands],
        out_specs=tuple(whole(o) for o in out_shape),
        scratch_shapes=[pltpu.VMEM((W, cols), F32)],
        compiler_params=params(32),
        cost_estimate=cost(12 * W * W * cols, 4 * W * (12 * cols + 6 * W)),
        name="lower",
    )(flags, pos, *zts, low, *operands)


def device_at(z, y, x, c):
    return ((z * CHIPS_Y + y) * CHIPS_X + x) * CORES + c


def moves(f):
    pairs = []
    for z in range(CHIPS_Z):
        for y in range(CHIPS_Y):
            for x in range(CHIPS_X):
                for c in range(CORES):
                    pairs.append((device_at(z, y, x, c), device_at(*f(z, y, x, c))))
    return pairs


ALONG_Z = moves(lambda z, y, x, c: ((z + 1) % CHIPS_Z, y, x, c))
AGAINST_Z = moves(lambda z, y, x, c: ((z - 1) % CHIPS_Z, y, x, c))
DIAGONAL = moves(lambda z, y, x, c: (z, 1 - y, 1 - x, c))
Z_BY = [moves(lambda z, y, x, c, s=s: ((z + s) % CHIPS_Z, y, x, c)) for s in range(CHIPS_Z)]
ALONG_Y = moves(lambda z, y, x, c: (z, 1 - y, x, c))
ALONG_X = moves(lambda z, y, x, c: (z, y, 1 - x, c))
ALONG_C = moves(lambda z, y, x, c: (z, y, x, 1 - c))


def move(x, pairs):
    return lax.ppermute(x, "blk", pairs)


def sync(values, after):
    values, after = list(values), list(after)
    anywhere = pl.BlockSpec(memory_space=pl.ANY)
    return pl.pallas_call(
        lambda *refs: None,
        out_shape=[jax.ShapeDtypeStruct(x.shape, x.dtype) for x in values],
        in_specs=[anywhere] * (len(values) + len(after)),
        out_specs=[anywhere] * len(values),
        input_output_aliases={i: i for i in range(len(values))},
        compiler_params=params(1),
        cost_estimate=cost(0, 0),
        name="sync",
    )(*values, *after)


def other_core(lines):
    return [move(a, ALONG_C) for a in lines]


def piece_order(me):
    c = me % CORES
    x = me // CORES % CHIPS_X
    y = me // (CORES * CHIPS_X) % CHIPS_Y
    z = me // (CORES * CHIPS_X * CHIPS_Y)
    def chip(yy, xx, cc):
        return [
            device_at((z + CHIPS_Z - back) % CHIPS_Z, yy, xx, cc) for back in range(CHIPS_Z)
        ]

    near, corner = [], []
    for cc in (c, 1 - c):
        near.append(chip(y, x, cc) + chip(y, 1 - x, cc) + chip(1 - y, x, cc))
        corner.append(chip(1 - y, 1 - x, cc))
    return jnp.stack(near[0] + near[1] + corner[0] + corner[1]).astype(jnp.int32)


def summed(me, share):
    core, place, z = me % CORES, me // CORES % (CHIPS_Y * CHIPS_X), me // device_at(1, 0, 0, 0)

    def rows(x, at, dim=0):
        return lax.dynamic_index_in_dim(x, at, dim, keepdims=False)

    share = rows(share, core, 2) + move(rows(share, 1 - core, 2), ALONG_C)
    share = (
        rows(share, place)
        + move(rows(share, place ^ 1), ALONG_X)
        + move(rows(share, place ^ CHIPS_X), ALONG_Y)
        + move(rows(share, place ^ (1 + CHIPS_X)), DIAGONAL)
    )
    total = rows(share, z)
    for step in range(1, CHIPS_Z):
        total += move(rows(share, (z + step) % CHIPS_Z), Z_BY[step])
    return total


def one_group(sigma_anc, panels, diag_inv, scaled_parent_panel, struct_upper, struct_lower):
    me = lax.axis_index("blk")
    pos = piece_order(me)
    own_blocks = 2 * me + jnp.arange(2, dtype=jnp.int32)
    on_first = (me == 0).astype(jnp.int32)[None]

    def owns(row):
        return jnp.any(row[None, :] == own_blocks[:, None], axis=1).astype(jnp.int32)

    def finish_upper(j, zt):
        return upper(j, upper_flags[j], pos, zt, pieces, diag_inv, scaled_parent_panel)

    def both_cores(lines):
        return lines + other_core(lines)

    low_blocks = struct_lower.reshape(SLOTS)
    pieces = transposed_pieces(panels, 0, 4)
    spread = lax.all_to_all(pieces, "blk", 0, 0, tiled=True).reshape(-1, SUB, W)

    def offsets(blocks, which):
        return 8 * (blocks // 2) + 2 * which + blocks % 2

    which = jnp.arange(LOWER_NODES_2, dtype=jnp.int32)[:, None]
    upper_flags = [
        jnp.concatenate([owns(struct_upper[j]), owns(struct_lower[j]), on_first])
        for j in range(UPPER_NODES_1)
    ]
    lower_flags = jnp.concatenate([owns(struct_lower[0]), owns(struct_lower[1])])
    own = picked(offsets(struct_upper, which).reshape(-1), spread)
    own_low = picked(offsets(struct_lower, UPPER_NODES_1 + which).reshape(-1), spread)
    small = upper_flags + [lower_flags, pos, low_blocks]
    (own,) = sync([own], small)

    lines, xs, ys = [own], [], []
    far_lines, far_xs, far_ys = [], [], []
    for step in range(CHIPS_Z - 1):
        moved = [move(lines[-1], d) for d in (ALONG_Z, ALONG_X, ALONG_Y)]
        swapped = [move(lines[-1], ALONG_C)]
        if step > 0:
            swapped.append(move(xs[-1] if step == 1 else ys[0], ALONG_C))
        if step == 0:
            line, x, y, own_low = sync(moved + [own_low], swapped)
        else:
            line, x, y = sync(moved, swapped)
        lines, xs, ys = lines + [line], xs + [x], ys + [y]
        far_lines.append(swapped[0])
        if step > 0:
            (far_xs if step == 1 else far_ys).append(swapped[1])
    moved = [
        move(lines[3], ALONG_X),
        move(lines[3], ALONG_Y),
        move(ys[0], ALONG_X),
        move(xs[1], ALONG_Y),
        move(own_low, ALONG_Z),
    ]
    swapped = other_core([lines[3], xs[1], ys[1], xs[2], ys[2]])
    x3, y3, d0, d1, behind = sync(moved, swapped)
    far_lines.append(swapped[0])
    far_xs += swapped[1::2]
    far_ys += swapped[2::2]
    xs, ys = xs + [x3], ys + [y3]
    moved = [
        move(ys[2], ALONG_X),
        move(xs[3], ALONG_Y),
        move(behind, ALONG_Z),
        move(own_low, AGAINST_Z),
        jnp.concatenate([own_low, behind]),
    ]
    swapped = other_core([xs[3], ys[3], d0, d1])
    d2, d3, across, before, first_pair = sync(moved, swapped)
    far_xs.append(swapped[0])
    far_ys.append(swapped[1])
    gathered = lines + xs + ys + far_lines + far_xs + far_ys
    gathered += [d0, d1, d2, d3, swapped[2], swapped[3], *other_core([d2, d3])]

    s = [first_pair, jnp.concatenate([across, before])]
    tx = [move(a, ALONG_X) for a in s]
    ty = [move(a, ALONG_Y) for a in s]
    zt0 = product(struct_upper[0], sigma_anc, gathered, 1, 0)
    zt1 = product(struct_upper[1], sigma_anc, gathered, 1, 1)
    far_s = other_core(s)
    *sides, zt0, zt1 = sync([*tx, *ty, zt0, zt1], far_s)
    tx, ty = sides[:2], sides[2:]
    corner = [move(ty[0], ALONG_X), move(tx[1], ALONG_Y)]
    up0, up1 = finish_upper(0, zt0), finish_upper(1, zt1)
    near = s + sides + far_s + other_core(sides)
    corner = list(sync(corner, [up0[2], up1[2], *near]))
    zt = product(low_blocks, sigma_anc, near + both_cores(corner), LOWER_NODES_2, mib=60)
    panel, late = lower(lower_flags, pos, [zt], pieces, (up0, up1))
    by_device = (CHIPS_Z, CHIPS_Y * CHIPS_X, CORES, -1, W)
    diag_share = jnp.concatenate([up0[2], up1[2], late]).reshape(by_device)
    parent_share = jnp.concatenate([up0[3], up1[3]]).reshape(by_device)
    total = summed(me, jnp.swapaxes(jnp.concatenate([diag_share, parent_share], axis=3), 0, 1))
    diag_rows = diag_share.shape[3]
    return panel, total[:diag_rows], total[diag_rows:]


def block_table(struct_upper, struct_lower, blocks):
    ids = jnp.arange(blocks, dtype=jnp.int32)
    upper = jnp.any(struct_upper[:, :, None] == ids[None, None, :], axis=1)
    lower = jnp.any(struct_lower[:, :, None] == ids[None, None, :], axis=1)
    return jnp.concatenate([upper, lower], axis=0).astype(jnp.float32)


def row_mask(table, first_row, count):
    blocks = table.shape[1]
    rows = first_row + jnp.arange(count, dtype=jnp.int32)
    membership_grid = (
        (rows // NODE_WIDTH)[:, None] == jnp.arange(blocks, dtype=jnp.int32)[None, :]
    ).astype(jnp.float32)
    return jnp.dot(
        membership_grid, table.T, precision=HIGH_ACCURACY, preferred_element_type=jnp.float32
    )


def strip_summands(reciprocal_lines, array_lines, membership_grid, stacked_arrays):
    count = reciprocal_lines.shape[0]
    upper_width_1 = UPPER_NODES_1 * NODE_WIDTH
    matrix_columns = jnp.repeat(array_lines, NODE_WIDTH, axis=1)
    g_up = -(matrix_columns[:, :upper_width_1] * reciprocal_lines[:, :upper_width_1])
    collected_elder_share = jnp.einsum(
        "rjw,cj->rcw",
        g_up.reshape(count, UPPER_NODES_1, NODE_WIDTH),
        membership_grid,
        precision=HIGH_ACCURACY,
    )
    resolved_bottom_share = matrix_columns[:, upper_width_1:].reshape(
        count, LOWER_NODES_2, NODE_WIDTH
    ) * (
        jnp.einsum("odf,dfy->ody", collected_elder_share, stacked_arrays, precision=HIGH_ACCURACY)
        + reciprocal_lines[:, upper_width_1:].reshape(count, LOWER_NODES_2, NODE_WIDTH)
    )
    strip_result = jnp.concatenate(
        [g_up, -resolved_bottom_share.reshape(count, LOWER_NODES_2 * NODE_WIDTH)], axis=1
    )
    return (strip_result, collected_elder_share, resolved_bottom_share)


def block_sums(urows, reciprocal_lines, collected_elder_share, resolved_bottom_share):
    count = urows.shape[0]
    upper_width_1 = UPPER_NODES_1 * NODE_WIDTH
    u_up = urows[:, :upper_width_1].reshape(count, UPPER_NODES_1, NODE_WIDTH)
    u_low = urows[:, upper_width_1:].reshape(count, LOWER_NODES_2, NODE_WIDTH)
    amat = jnp.einsum(
        "rjw,rjv->jwv",
        u_up,
        reciprocal_lines[:, :upper_width_1].reshape(count, UPPER_NODES_1, NODE_WIDTH),
        precision=HIGH_ACCURACY,
    )
    block_matrix = jnp.einsum("rcw,rcv->cwv", u_low, collected_elder_share, precision=HIGH_ACCURACY)
    extra_matrix = jnp.einsum("rcw,rcv->cwv", u_low, resolved_bottom_share, precision=HIGH_ACCURACY)
    return jnp.concatenate([amat, block_matrix, extra_matrix], axis=0)


def per_device(sigma_anc, panels, diag_inv, scaled_parent_panel, struct_upper, struct_lower):
    rows_grp, cols_dev = sigma_anc.shape
    rows_dev = panels.shape[0]
    grp_count = lax.axis_size("grp")
    blk_count = lax.axis_size("blk")
    grp_pos = lax.axis_index("grp")
    blk_pos = lax.axis_index("blk")
    blocks = cols_dev * blk_count // NODE_WIDTH
    table = block_table(struct_upper, struct_lower, blocks)
    parent_ids = jnp.arange(LOWER_NODES_2, dtype=jnp.int32) % UPPER_NODES_1
    membership_grid = (
        parent_ids[:, None] == jnp.arange(UPPER_NODES_1, dtype=jnp.int32)[None, :]
    ).astype(jnp.float32)
    stacked_arrays = scaled_parent_panel.reshape(LOWER_NODES_2, NODE_WIDTH, NODE_WIDTH)
    first_in = grp_pos * rows_grp + blk_pos * rows_dev
    upanel = panels * jnp.repeat(row_mask(table, first_in, rows_dev), NODE_WIDTH, axis=1)
    grouped = lax.all_gather(upanel, "blk", axis=0, tiled=True)
    partial_value = lax.dot_general(
        sigma_anc,
        grouped,
        (((0,), (0,)), ((), ())),
        precision=HIGH_ACCURACY,
        preferred_element_type=jnp.float32,
    )
    share = cols_dev // grp_count
    col_first = blk_pos * cols_dev
    root = col_first // rows_grp
    offset = jnp.clip(col_first - grp_pos * rows_grp, 0, rows_grp - cols_dev)
    own_first = col_first + grp_pos * share
    owned_mask = row_mask(table, own_first, share)
    nterms = UPPER_NODES_1 + 2 * LOWER_NODES_2
    inverse_columns = lax.psum(partial_value, "grp")
    inverse_owned = lax.dynamic_slice_in_dim(inverse_columns, grp_pos * share, share, 0)
    strip_result, collected_elder_share, resolved_bottom_share = strip_summands(
        inverse_owned, owned_mask, membership_grid, stacked_arrays
    )

    def on_root():
        u_cols = lax.dynamic_slice_in_dim(grouped, offset, cols_dev, 0)
        complete_mask = row_mask(table, col_first, cols_dev)
        discarded_result, collected_entire_factor, resolved_entire_factor = strip_summands(
            inverse_columns, complete_mask, membership_grid, stacked_arrays
        )
        return block_sums(u_cols, inverse_columns, collected_entire_factor, resolved_entire_factor)

    def off_root():
        return jnp.zeros((nterms, NODE_WIDTH, NODE_WIDTH), jnp.float32)

    terms = lax.cond(grp_pos == root, on_root, off_root)
    summed = lax.psum(terms, ("grp", "blk"))
    amat = summed[:UPPER_NODES_1]
    block_matrix = summed[UPPER_NODES_1 : UPPER_NODES_1 + LOWER_NODES_2]
    extra_matrix = summed[UPPER_NODES_1 + LOWER_NODES_2 :]
    diagonal_matrices = diag_inv.reshape(UPPER_NODES_1 + LOWER_NODES_2, NODE_WIDTH, NODE_WIDTH)
    s_up = diagonal_matrices[:UPPER_NODES_1] + amat
    parent_selection = jnp.einsum("cj,jwv->cwv", membership_grid, s_up, precision=HIGH_ACCURACY)
    solved_parent = jnp.einsum(
        "ghz,gzs->ghs", parent_selection, stacked_arrays, precision=HIGH_ACCURACY
    ) + jnp.transpose(block_matrix, (0, 2, 1))
    lower_selection = (
        diagonal_matrices[UPPER_NODES_1:]
        + jnp.einsum("lmt,lmx->ltx", stacked_arrays, solved_parent, precision=HIGH_ACCURACY)
        + extra_matrix
    )
    whole_diag = jnp.concatenate([s_up, lower_selection], axis=0).reshape(
        (UPPER_NODES_1 + LOWER_NODES_2) * NODE_WIDTH, NODE_WIDTH
    )
    whole_parent = -solved_parent.reshape(LOWER_NODES_2 * NODE_WIDTH, NODE_WIDTH)
    diag_rows = (UPPER_NODES_1 + LOWER_NODES_2) * NODE_WIDTH // blk_count
    parent_rows = LOWER_NODES_2 * NODE_WIDTH // blk_count
    cov_diag = lax.dynamic_slice_in_dim(whole_diag, blk_pos * diag_rows, diag_rows, 0)
    cov_parent = lax.dynamic_slice_in_dim(whole_parent, blk_pos * parent_rows, parent_rows, 0)
    return (strip_result, cov_diag, cov_parent)


def solution(mesh):
    single = mesh.shape["grp"] == 1 and mesh.shape["blk"] == PIECES
    return jax.shard_map(
        one_group if single else per_device,
        mesh=mesh,
        in_specs=(P("grp", "blk"), P(("grp", "blk"), None), P(), P(), P(), P()),
        out_specs=(P(("blk", "grp"), None), P("blk", None), P("blk", None)),
        check_vma=False,
    )
```

```python
import jax
import jax.numpy as jnp
from jax import lax
from jax.experimental import pallas as pl
from jax.experimental.pallas import tpu as pltpu
from jax.sharding import PartitionSpec as P

NODE_WIDTH = 256
UPPER_NODES_1 = 2
LOWER_NODES_2 = 2
F32 = jnp.float32
BF16 = jnp.bfloat16


HIGH_ACCURACY = lax.Precision.HIGHEST


CHIPS_Z, CHIPS_Y, CHIPS_X, CORES = 4, 2, 2, 2
PIECES = CHIPS_Z * CHIPS_Y * CHIPS_X * CORES
SUB = NODE_WIDTH // PIECES
SLOTS = 32
PER_STEP = 4
W = NODE_WIDTH


def params(mib):
    return pltpu.CompilerParams(vmem_limit_bytes=mib * 1024 * 1024)


def split(x):
    hi = x.astype(BF16)
    return hi, (x - hi.astype(F32)).astype(BF16)


def dot3(a, b):
    a_hi, a_lo = split(a)
    b_hi, b_lo = split(b)
    small = jnp.dot(a_lo, b_hi, preferred_element_type=F32) + jnp.dot(
        a_hi, b_lo, preferred_element_type=F32
    )
    return jnp.dot(a_hi, b_hi, preferred_element_type=F32) + small


def cost(flops, nbytes):
    return pl.CostEstimate(flops=flops, bytes_accessed=nbytes, transcendentals=0)


def transpose_body(x_ref, o_ref):
    for c in range(o_ref.shape[1]):
        for rb in range(2):
            t = x_ref[rb * W : (rb + 1) * W, c * W : (c + 1) * W].T
            o_ref[:, c, rb] = t.reshape(PIECES, SUB, W)


def transposed_pieces(panels, first, count):
    shape = (PIECES, count, 2, SUB, W)
    return pl.pallas_call(
        transpose_body,
        out_shape=jax.ShapeDtypeStruct(shape, F32),
        grid=(1,),
        in_specs=[pl.BlockSpec((2 * W, count * W), lambda i: (0, first // count))],
        out_specs=pl.BlockSpec(shape, lambda i: (0, 0, 0, 0, 0)),
        compiler_params=params(16),
        cost_estimate=cost(0, 4 * panels.size * count // 2),
        name="transposed_pieces",
    )(panels)


def pick_body(idx_ref, a_ref, o_ref):
    for k in range(o_ref.shape[1]):
        o_ref[0, k] = a_ref[idx_ref[k]]


def picked(idx, a):
    return pl.pallas_call(
        pick_body,
        out_shape=jax.ShapeDtypeStruct((1, idx.shape[0], SUB, W), F32),
        in_specs=[
            pl.BlockSpec(memory_space=pltpu.SMEM),
            pl.BlockSpec(memory_space=pltpu.VMEM),
        ],
        out_specs=pl.BlockSpec(memory_space=pltpu.VMEM),
        compiler_params=params(16),
        cost_estimate=cost(0, 4 * (a.size + idx.size * SUB * W)),
        name="picked",
    )(idx, a)


def product_body(accs, idx_ref, *refs):
    sig, lines, o_ref = refs[:PER_STEP], refs[PER_STEP:-1], refs[-1]
    step = pl.program_id(0)
    per_acc = pl.num_programs(0) // accs
    left = []
    for q in range(PER_STEP):
        left.append(jnp.concatenate([r[:, q].reshape(-1, W) for r in lines], axis=0))
    value = dot3(jnp.concatenate(left, axis=1), jnp.concatenate([r[...] for r in sig], axis=0))

    @pl.when(lax.rem(step, per_acc) == 0)
    def _():
        o_ref[0] = value

    @pl.when(lax.rem(step, per_acc) != 0)
    def _():
        o_ref[0] += value


def product(idx, sigma, pieces, accs, chunk=0, mib=18):
    steps = SLOTS // PER_STEP
    cols = sigma.shape[1]
    rows = SUB * sum(p.shape[0] for p in pieces)

    def sig_spec(q):
        return pl.BlockSpec((W, cols), lambda i, idx, q=q: (idx[i * PER_STEP + q], 0))

    piece_specs = [
        pl.BlockSpec((p.shape[0], PER_STEP, SUB, W), lambda i, idx: (0, i + chunk * steps, 0, 0))
        for p in pieces
    ]
    return pl.pallas_call(
        lambda *refs: product_body(accs, *refs),
        out_shape=jax.ShapeDtypeStruct((accs, rows, cols), F32),
        grid_spec=pltpu.PrefetchScalarGridSpec(
            num_scalar_prefetch=1,
            grid=(steps,),
            in_specs=[sig_spec(q) for q in range(PER_STEP)] + piece_specs,
            out_specs=pl.BlockSpec((1, rows, cols), lambda i, idx: (lax.div(i * accs, steps), 0, 0)),
        ),
        compiler_params=params(mib),
        cost_estimate=cost(6 * SLOTS * rows * W * cols, 4 * SLOTS * W * (cols + rows)),
        name="product",
    )(idx, *([sigma] * PER_STEP), *pieces)


def row_flags(rows, lo, hi):
    top = lax.broadcasted_iota(jnp.int32, (rows, 1), 0) < W
    return jnp.where(top, lo.astype(F32), hi.astype(F32))


def local_lines(ref, c):
    return jnp.concatenate([ref[:, c, rb].reshape(W, W) for rb in range(2)], axis=1)


def in_order(pos_ref, zt_refs, c, scratch):
    g = 0
    for ref in zt_refs:
        for row in range(0, ref.shape[1], SUB):
            at = pl.multiple_of(pos_ref[g] * SUB, SUB)
            scratch[pl.ds(at, SUB), :] = ref[c, row : row + SUB, :]
            g += 1
    return scratch[...].T


def upper_body(flag_ref, pos_ref, zt_ref, up_ref, low_ref, diag_ref, low_diag_ref, v_ref, *outs):
    g_ref, gv_ref, a_ref, yp_ref, l_ref, scratch = outs[-6:]
    z = in_order(pos_ref, [zt_ref], 0, scratch)
    g = -z * row_flags(z.shape[0], flag_ref[0], flag_ref[1])
    g_ref[...] = g
    on_first = flag_ref[4].astype(F32)
    a = diag_ref[...] * on_first - dot3(local_lines(up_ref, 0), g)
    a_ref[...] = a
    below = g * row_flags(z.shape[0], flag_ref[2], flag_ref[3])
    gv = dot3(below, v_ref[...])
    gv_ref[...] = gv
    u = local_lines(low_ref, 0)
    yp = dot3(a, v_ref[...]) + dot3(u, below).T
    yp_ref[...] = -yp
    l_ref[...] = dot3(v_ref[...].T, yp) + dot3(u, gv) + low_diag_ref[...] * on_first


def upper(j, flags, pos, zt, pieces, diag, v, panel):
    cols = zt.shape[2]
    square = jax.ShapeDtypeStruct((W, W), F32)
    tall = jax.ShapeDtypeStruct((cols, W), F32)
    def whole(x):
        return pl.BlockSpec(x.shape, lambda i: (0,) * x.ndim)

    def own(s):
        return pl.BlockSpec((PIECES, 1, 2, SUB, W), lambda i: (0, s, 0, 0, 0))

    def block(s):
        return pl.BlockSpec((W, W), lambda i: (s, 0))

    out_shape = (jax.ShapeDtypeStruct((cols, 4 * W), F32), tall, square, square, square)
    before = [] if panel is None else [panel]
    return pl.pallas_call(
        upper_body,
        out_shape=out_shape,
        grid=(1,),
        in_specs=[pl.BlockSpec(memory_space=pltpu.SMEM)] * 2
        + [whole(zt), own(j), own(UPPER_NODES_1 + j), block(j), block(UPPER_NODES_1 + j), block(j)]
        + [pl.BlockSpec(memory_space=pl.ANY)] * len(before),
        out_specs=(pl.BlockSpec((cols, W), lambda i: (0, j)), *(whole(o) for o in out_shape[1:])),
        input_output_aliases={8: 0} if before else {},
        scratch_shapes=[pltpu.VMEM((W, cols), F32)],
        compiler_params=params(24),
        cost_estimate=cost(24 * W * W * (cols + W), 4 * W * (6 * cols + 8 * W)),
        name="upper",
    )(flags, pos, zt, pieces, pieces, diag, diag, v, *before)


def lower_body(parts, flag_ref, pos_ref, *refs):
    zt_refs = refs[:parts]
    low_ref, gv0, gv1, l0, l1, _, panel_ref, late_ref, scratch = refs[parts:]
    for c, (gv_ref, l_ref) in enumerate(((gv0, l0), (gv1, l1))):
        z = in_order(pos_ref, zt_refs, c, scratch)
        z = z * row_flags(z.shape[0], flag_ref[2 * c], flag_ref[2 * c + 1])
        panel_ref[:, c * W : (c + 1) * W] = -(gv_ref[...] + z)
        late_ref[c * W : (c + 1) * W, :] = l_ref[...] + dot3(local_lines(low_ref, c), z)


def lower(flags, pos, zts, low, ups):
    cols = zts[0].shape[2]
    operands = [ups[j][i] for i in (1, 4) for j in range(UPPER_NODES_1)]
    def whole(x):
        return pl.BlockSpec(x.shape, lambda i: (0,) * x.ndim)

    out_shape = (
        jax.ShapeDtypeStruct((cols, 4 * W), F32),
        jax.ShapeDtypeStruct((LOWER_NODES_2 * W, W), F32),
    )
    return pl.pallas_call(
        lambda *refs: lower_body(len(zts), *refs),
        out_shape=out_shape,
        grid=(1,),
        in_specs=[pl.BlockSpec(memory_space=pltpu.SMEM)] * 2
        + [whole(z) for z in zts]
        + [pl.BlockSpec((PIECES, LOWER_NODES_2, 2, SUB, W), lambda i: (0, 1, 0, 0, 0))]
        + [whole(o) for o in operands]
        + [pl.BlockSpec(memory_space=pl.ANY)],
        out_specs=(pl.BlockSpec((cols, 2 * W), lambda i: (0, 1)), whole(out_shape[1])),
        input_output_aliases={3 + len(zts) + len(operands): 0},
        scratch_shapes=[pltpu.VMEM((W, cols), F32)],
        compiler_params=params(32),
        cost_estimate=cost(12 * W * W * cols, 4 * W * (12 * cols + 6 * W)),
        name="lower",
    )(flags, pos, *zts, low, *operands, ups[1][0])


def device_at(z, y, x, c):
    return ((z * CHIPS_Y + y) * CHIPS_X + x) * CORES + c


def moves(f):
    pairs = []
    for z in range(CHIPS_Z):
        for y in range(CHIPS_Y):
            for x in range(CHIPS_X):
                for c in range(CORES):
                    pairs.append((device_at(z, y, x, c), device_at(*f(z, y, x, c))))
    return pairs


ALONG_Z = moves(lambda z, y, x, c: ((z + 1) % CHIPS_Z, y, x, c))
AGAINST_Z = moves(lambda z, y, x, c: ((z - 1) % CHIPS_Z, y, x, c))
DIAGONAL = moves(lambda z, y, x, c: (z, 1 - y, 1 - x, c))
Z_BY = [moves(lambda z, y, x, c, s=s: ((z + s) % CHIPS_Z, y, x, c)) for s in range(CHIPS_Z)]
ALONG_Y = moves(lambda z, y, x, c: (z, 1 - y, x, c))
ALONG_X = moves(lambda z, y, x, c: (z, y, 1 - x, c))
ALONG_C = moves(lambda z, y, x, c: (z, y, x, 1 - c))


def move(x, pairs):
    return lax.ppermute(x, "blk", pairs)


def sync(values, after):
    values, after = list(values), list(after)
    anywhere = pl.BlockSpec(memory_space=pl.ANY)
    return pl.pallas_call(
        lambda *refs: None,
        out_shape=[jax.ShapeDtypeStruct(x.shape, x.dtype) for x in values],
        in_specs=[anywhere] * (len(values) + len(after)),
        out_specs=[anywhere] * len(values),
        input_output_aliases={i: i for i in range(len(values))},
        compiler_params=params(1),
        cost_estimate=cost(0, 0),
        name="sync",
    )(*values, *after)


def other_core(lines):
    return [move(a, ALONG_C) for a in lines]


def piece_order(me):
    c = me % CORES
    x = me // CORES % CHIPS_X
    y = me // (CORES * CHIPS_X) % CHIPS_Y
    z = me // (CORES * CHIPS_X * CHIPS_Y)
    def chip(yy, xx, cc):
        return [
            device_at((z + CHIPS_Z - back) % CHIPS_Z, yy, xx, cc) for back in range(CHIPS_Z)
        ]

    near, corner = [], []
    for cc in (c, 1 - c):
        near.append(chip(y, x, cc) + chip(y, 1 - x, cc) + chip(1 - y, x, cc))
        corner.append(chip(1 - y, 1 - x, cc))
    return jnp.stack(near[0] + near[1] + corner[0] + corner[1]).astype(jnp.int32)


def summed(me, share):
    core, place, z = me % CORES, me // CORES % (CHIPS_Y * CHIPS_X), me // device_at(1, 0, 0, 0)

    def rows(x, at, dim=0):
        return lax.dynamic_index_in_dim(x, at, dim, keepdims=False)

    share = rows(share, core, 2) + move(rows(share, 1 - core, 2), ALONG_C)
    share = (
        rows(share, place)
        + move(rows(share, place ^ 1), ALONG_X)
        + move(rows(share, place ^ CHIPS_X), ALONG_Y)
        + move(rows(share, place ^ (1 + CHIPS_X)), DIAGONAL)
    )
    total = rows(share, z)
    for step in range(1, CHIPS_Z):
        total += move(rows(share, (z + step) % CHIPS_Z), Z_BY[step])
    return total


def one_group(sigma_anc, panels, diag_inv, scaled_parent_panel, struct_upper, struct_lower):
    me = lax.axis_index("blk")
    pos = piece_order(me)
    own_blocks = 2 * me + jnp.arange(2, dtype=jnp.int32)
    on_first = (me == 0).astype(jnp.int32)[None]

    def owns(row):
        return jnp.any(row[None, :] == own_blocks[:, None], axis=1).astype(jnp.int32)

    def finish_upper(j, zt, panel):
        return upper(j, upper_flags[j], pos, zt, pieces, diag_inv, scaled_parent_panel, panel)

    def both_cores(lines):
        return lines + other_core(lines)

    low_blocks = struct_lower.reshape(SLOTS)
    pieces = transposed_pieces(panels, 0, 4)
    spread = lax.all_to_all(pieces, "blk", 0, 0, tiled=True).reshape(-1, SUB, W)

    def offsets(blocks, which):
        return 8 * (blocks // 2) + 2 * which + blocks % 2

    which = jnp.arange(LOWER_NODES_2, dtype=jnp.int32)[:, None]
    upper_flags = [
        jnp.concatenate([owns(struct_upper[j]), owns(struct_lower[j]), on_first])
        for j in range(UPPER_NODES_1)
    ]
    lower_flags = jnp.concatenate([owns(struct_lower[0]), owns(struct_lower[1])])
    own = picked(offsets(struct_upper, which).reshape(-1), spread)
    own_low = picked(offsets(struct_lower, UPPER_NODES_1 + which).reshape(-1), spread)
    small = upper_flags + [lower_flags, pos, low_blocks]
    (own,) = sync([own], small)

    lines, xs, ys = [own], [], []
    far_lines, far_xs, far_ys = [], [], []
    for step in range(CHIPS_Z - 1):
        moved = [move(lines[-1], d) for d in (ALONG_Z, ALONG_X, ALONG_Y)]
        swapped = [move(lines[-1], ALONG_C)]
        if step > 0:
            swapped.append(move(xs[-1] if step == 1 else ys[0], ALONG_C))
        if step == 0:
            line, x, y, own_low = sync(moved + [own_low], swapped)
        else:
            line, x, y = sync(moved, swapped)
        lines, xs, ys = lines + [line], xs + [x], ys + [y]
        far_lines.append(swapped[0])
        if step > 0:
            (far_xs if step == 1 else far_ys).append(swapped[1])
    moved = [
        move(lines[3], ALONG_X),
        move(lines[3], ALONG_Y),
        move(ys[0], ALONG_X),
        move(xs[1], ALONG_Y),
        move(own_low, ALONG_Z),
    ]
    swapped = other_core([lines[3], xs[1], ys[1], xs[2], ys[2]])
    x3, y3, d0, d1, behind = sync(moved, swapped)
    far_lines.append(swapped[0])
    far_xs += swapped[1::2]
    far_ys += swapped[2::2]
    xs, ys = xs + [x3], ys + [y3]
    moved = [
        move(ys[2], ALONG_X),
        move(xs[3], ALONG_Y),
        move(behind, ALONG_Z),
        move(own_low, AGAINST_Z),
        jnp.concatenate([own_low, behind]),
    ]
    swapped = other_core([xs[3], ys[3], d0, d1])
    d2, d3, across, before, first_pair = sync(moved, swapped)
    far_xs.append(swapped[0])
    far_ys.append(swapped[1])
    gathered = lines + xs + ys + far_lines + far_xs + far_ys
    gathered += [d0, d1, d2, d3, swapped[2], swapped[3], *other_core([d2, d3])]

    s = [first_pair, jnp.concatenate([across, before])]
    tx = [move(a, ALONG_X) for a in s]
    ty = [move(a, ALONG_Y) for a in s]
    zt0 = product(struct_upper[0], sigma_anc, gathered, 1, 0)
    zt1 = product(struct_upper[1], sigma_anc, gathered, 1, 1)
    far_s = other_core(s)
    *sides, zt0, zt1 = sync([*tx, *ty, zt0, zt1], far_s)
    tx, ty = sides[:2], sides[2:]
    corner = [move(ty[0], ALONG_X), move(tx[1], ALONG_Y)]
    up0 = finish_upper(0, zt0, None)
    up1 = finish_upper(1, zt1, up0[0])
    near = s + sides + far_s + other_core(sides)
    corner = list(sync(corner, [up0[2], up1[2], *near]))
    zt = product(low_blocks, sigma_anc, near + both_cores(corner), LOWER_NODES_2, mib=60)
    panel, late = lower(lower_flags, pos, [zt], pieces, (up0, up1))
    by_device = (CHIPS_Z, CHIPS_Y * CHIPS_X, CORES, -1, W)
    diag_share = jnp.concatenate([up0[2], up1[2], late]).reshape(by_device)
    parent_share = jnp.concatenate([up0[3], up1[3]]).reshape(by_device)
    total = summed(me, jnp.swapaxes(jnp.concatenate([diag_share, parent_share], axis=3), 0, 1))
    diag_rows = diag_share.shape[3]
    return panel, total[:diag_rows], total[diag_rows:]


def block_table(struct_upper, struct_lower, blocks):
    ids = jnp.arange(blocks, dtype=jnp.int32)
    upper = jnp.any(struct_upper[:, :, None] == ids[None, None, :], axis=1)
    lower = jnp.any(struct_lower[:, :, None] == ids[None, None, :], axis=1)
    return jnp.concatenate([upper, lower], axis=0).astype(jnp.float32)


def row_mask(table, first_row, count):
    blocks = table.shape[1]
    rows = first_row + jnp.arange(count, dtype=jnp.int32)
    membership_grid = (
        (rows // NODE_WIDTH)[:, None] == jnp.arange(blocks, dtype=jnp.int32)[None, :]
    ).astype(jnp.float32)
    return jnp.dot(
        membership_grid, table.T, precision=HIGH_ACCURACY, preferred_element_type=jnp.float32
    )


def strip_summands(reciprocal_lines, array_lines, membership_grid, stacked_arrays):
    count = reciprocal_lines.shape[0]
    upper_width_1 = UPPER_NODES_1 * NODE_WIDTH
    matrix_columns = jnp.repeat(array_lines, NODE_WIDTH, axis=1)
    g_up = -(matrix_columns[:, :upper_width_1] * reciprocal_lines[:, :upper_width_1])
    collected_elder_share = jnp.einsum(
        "rjw,cj->rcw",
        g_up.reshape(count, UPPER_NODES_1, NODE_WIDTH),
        membership_grid,
        precision=HIGH_ACCURACY,
    )
    resolved_bottom_share = matrix_columns[:, upper_width_1:].reshape(
        count, LOWER_NODES_2, NODE_WIDTH
    ) * (
        jnp.einsum("odf,dfy->ody", collected_elder_share, stacked_arrays, precision=HIGH_ACCURACY)
        + reciprocal_lines[:, upper_width_1:].reshape(count, LOWER_NODES_2, NODE_WIDTH)
    )
    strip_result = jnp.concatenate(
        [g_up, -resolved_bottom_share.reshape(count, LOWER_NODES_2 * NODE_WIDTH)], axis=1
    )
    return (strip_result, collected_elder_share, resolved_bottom_share)


def block_sums(urows, reciprocal_lines, collected_elder_share, resolved_bottom_share):
    count = urows.shape[0]
    upper_width_1 = UPPER_NODES_1 * NODE_WIDTH
    u_up = urows[:, :upper_width_1].reshape(count, UPPER_NODES_1, NODE_WIDTH)
    u_low = urows[:, upper_width_1:].reshape(count, LOWER_NODES_2, NODE_WIDTH)
    amat = jnp.einsum(
        "rjw,rjv->jwv",
        u_up,
        reciprocal_lines[:, :upper_width_1].reshape(count, UPPER_NODES_1, NODE_WIDTH),
        precision=HIGH_ACCURACY,
    )
    block_matrix = jnp.einsum("rcw,rcv->cwv", u_low, collected_elder_share, precision=HIGH_ACCURACY)
    extra_matrix = jnp.einsum("rcw,rcv->cwv", u_low, resolved_bottom_share, precision=HIGH_ACCURACY)
    return jnp.concatenate([amat, block_matrix, extra_matrix], axis=0)


def per_device(sigma_anc, panels, diag_inv, scaled_parent_panel, struct_upper, struct_lower):
    rows_grp, cols_dev = sigma_anc.shape
    rows_dev = panels.shape[0]
    grp_count = lax.axis_size("grp")
    blk_count = lax.axis_size("blk")
    grp_pos = lax.axis_index("grp")
    blk_pos = lax.axis_index("blk")
    blocks = cols_dev * blk_count // NODE_WIDTH
    table = block_table(struct_upper, struct_lower, blocks)
    parent_ids = jnp.arange(LOWER_NODES_2, dtype=jnp.int32) % UPPER_NODES_1
    membership_grid = (
        parent_ids[:, None] == jnp.arange(UPPER_NODES_1, dtype=jnp.int32)[None, :]
    ).astype(jnp.float32)
    stacked_arrays = scaled_parent_panel.reshape(LOWER_NODES_2, NODE_WIDTH, NODE_WIDTH)
    first_in = grp_pos * rows_grp + blk_pos * rows_dev
    upanel = panels * jnp.repeat(row_mask(table, first_in, rows_dev), NODE_WIDTH, axis=1)
    grouped = lax.all_gather(upanel, "blk", axis=0, tiled=True)
    partial_value = lax.dot_general(
        sigma_anc,
        grouped,
        (((0,), (0,)), ((), ())),
        precision=HIGH_ACCURACY,
        preferred_element_type=jnp.float32,
    )
    share = cols_dev // grp_count
    col_first = blk_pos * cols_dev
    root = col_first // rows_grp
    offset = jnp.clip(col_first - grp_pos * rows_grp, 0, rows_grp - cols_dev)
    own_first = col_first + grp_pos * share
    owned_mask = row_mask(table, own_first, share)
    nterms = UPPER_NODES_1 + 2 * LOWER_NODES_2
    inverse_columns = lax.psum(partial_value, "grp")
    inverse_owned = lax.dynamic_slice_in_dim(inverse_columns, grp_pos * share, share, 0)
    strip_result, collected_elder_share, resolved_bottom_share = strip_summands(
        inverse_owned, owned_mask, membership_grid, stacked_arrays
    )

    def on_root():
        u_cols = lax.dynamic_slice_in_dim(grouped, offset, cols_dev, 0)
        complete_mask = row_mask(table, col_first, cols_dev)
        discarded_result, collected_entire_factor, resolved_entire_factor = strip_summands(
            inverse_columns, complete_mask, membership_grid, stacked_arrays
        )
        return block_sums(u_cols, inverse_columns, collected_entire_factor, resolved_entire_factor)

    def off_root():
        return jnp.zeros((nterms, NODE_WIDTH, NODE_WIDTH), jnp.float32)

    terms = lax.cond(grp_pos == root, on_root, off_root)
    summed = lax.psum(terms, ("grp", "blk"))
    amat = summed[:UPPER_NODES_1]
    block_matrix = summed[UPPER_NODES_1 : UPPER_NODES_1 + LOWER_NODES_2]
    extra_matrix = summed[UPPER_NODES_1 + LOWER_NODES_2 :]
    diagonal_matrices = diag_inv.reshape(UPPER_NODES_1 + LOWER_NODES_2, NODE_WIDTH, NODE_WIDTH)
    s_up = diagonal_matrices[:UPPER_NODES_1] + amat
    parent_selection = jnp.einsum("cj,jwv->cwv", membership_grid, s_up, precision=HIGH_ACCURACY)
    solved_parent = jnp.einsum(
        "ghz,gzs->ghs", parent_selection, stacked_arrays, precision=HIGH_ACCURACY
    ) + jnp.transpose(block_matrix, (0, 2, 1))
    lower_selection = (
        diagonal_matrices[UPPER_NODES_1:]
        + jnp.einsum("lmt,lmx->ltx", stacked_arrays, solved_parent, precision=HIGH_ACCURACY)
        + extra_matrix
    )
    whole_diag = jnp.concatenate([s_up, lower_selection], axis=0).reshape(
        (UPPER_NODES_1 + LOWER_NODES_2) * NODE_WIDTH, NODE_WIDTH
    )
    whole_parent = -solved_parent.reshape(LOWER_NODES_2 * NODE_WIDTH, NODE_WIDTH)
    diag_rows = (UPPER_NODES_1 + LOWER_NODES_2) * NODE_WIDTH // blk_count
    parent_rows = LOWER_NODES_2 * NODE_WIDTH // blk_count
    cov_diag = lax.dynamic_slice_in_dim(whole_diag, blk_pos * diag_rows, diag_rows, 0)
    cov_parent = lax.dynamic_slice_in_dim(whole_parent, blk_pos * parent_rows, parent_rows, 0)
    return (strip_result, cov_diag, cov_parent)


def solution(mesh):
    single = mesh.shape["grp"] == 1 and mesh.shape["blk"] == PIECES
    return jax.shard_map(
        one_group if single else per_device,
        mesh=mesh,
        in_specs=(P("grp", "blk"), P(("grp", "blk"), None), P(), P(), P(), P()),
        out_specs=(P(("blk", "grp"), None), P("blk", None), P("blk", None)),
        check_vma=False,
    )
```
